256 devices in a mesh: dp: 8 (over x, core), expert: 32 (over z, y).
Axes of the slice: x: 4, y: 4, z: 8, core: 2. Of those that a mesh axis runs over, the one named last changes fastest.
Arguments:
- grad_out: bfloat16 [32768, 3584], P(('dp', 'expert')), may hold values from -1.5 to 1.5
- gate_probs: float32 [32768, 4], P(('dp', 'expert')), may hold values from 0.05 to 0.3
- expert_route: int32 [32768, 4], P(('dp', 'expert')), may hold values from 0 to 23, all different within a row; in each aligned block of 128 rows (0 to 127, 128 to 255, ...) at most 24 rows name the same one
- replica_pick: int32 [32768, 4], P(('dp', 'expert')), may hold values from 0 to 59
- slot_expert: int32 [32], replicated, may hold values from 0 to 23, as said below
- saved_hidden: bfloat16 [8, 32, 32, 1, 24, 1024], P('dp', 'expert'), may hold values from -6 to 6
- master: float32 [32, 1024, 3584], P('expert', 'dp'), as said below
- first_moment: bfloat16 [32, 1024, 3584], P('expert', 'dp'), as said below
- second_moment: bfloat16 [32, 1024, 3584], P('expert', 'dp'), as said below
Outputs:
- hidden_grad: bfloat16 [8, 32, 32, 1, 24, 1024], P('dp', 'expert')
- gate_grad: float32 [32768, 4], P(('dp', 'expert'))
- new_master: float32 [32, 1024, 3584], P('expert', 'dp')
- new_first: bfloat16 [32, 1024, 3584], P('expert', 'dp')
- new_second: bfloat16 [32, 1024, 3584], P('expert', 'dp')
The draws below stay inside these ranges and needn't reach their ends.
Inputs may be any that keep to these rules, and one draw needn't show every extreme that they name: `expert_route`: each row names 4 different experts; in the rows of one device no expert is named more than 24 times, a bound that some block reaches. `slot_expert`: every expert has at least one slot; experts 0 to 2 have two or more slots each, every other expert exactly one. `master`: slots holding the same expert hold equal values. `first_moment`: slots holding the same expert hold equal values. `second_moment`: slots holding the same expert hold equal values; all entries are positive.
All inputs are finite; a program needn't handle non-finite values.
Results may differ from the reference program's by a relative error of at most 0.017.
Values may be sent and summed in bfloat16 or wider, within the bound.
A program may use at most 128 MiB of HBM per device.

```python
import math
import jax
import jax.numpy as jnp
import numpy as np
from jax import lax

D = 3584
HID = 1024
TOPK = 4
HOT = 3
TOK_DEV = 128
SLOT_DEV = 1
N_SLOTS = 32
REPLICAS = 8
EXPERTS = 24
CAP = 24
TOKENS = 32768
N_DP = 8
N_EXPERT = 32


def placement_table(key):
    base_key = jax.random.fold_in(key, 11)
    extra_key = jax.random.fold_in(base_key, 1)
    order_key = jax.random.fold_in(base_key, 2)
    start_key = jax.random.fold_in(base_key, 3)
    start = jax.random.randint(start_key, (), 0, N_EXPERT).astype(jnp.int32)
    first_pos = start * SLOT_DEV
    second_pos = (start + 1) % N_EXPERT * SLOT_DEV
    third_pos = (start + N_EXPERT // 2) % N_EXPERT * SLOT_DEV
    extra = jax.random.randint(extra_key, (REPLICAS - HOT - 1,), 0, HOT).astype(jnp.int32)
    listed = jnp.concatenate([jnp.arange(1, EXPERTS, dtype=jnp.int32), jnp.arange(1, HOT, dtype=jnp.int32), extra])
    order = jax.random.permutation(order_key, N_SLOTS - 3)
    rest = listed[order].astype(jnp.int32)
    slot_ids = jnp.arange(N_SLOTS, dtype=jnp.int32)
    fixed = (slot_ids == first_pos) | (slot_ids == second_pos) | (slot_ids == third_pos)
    free_order = jnp.argsort(fixed.astype(jnp.int32), stable=True).astype(jnp.int32)
    table = jnp.zeros((N_SLOTS,), jnp.int32).at[free_order[:N_SLOTS - 3]].set(rest)
    return table.astype(jnp.int32)


def draw_slot_expert(key, part):
    return placement_table(key)


def draw_master(key, part):
    table = placement_table(key)
    value_key = jax.random.fold_in(key, 21)
    values = jax.random.normal(value_key, (EXPERTS, HID, D), jnp.float32) * D ** (-0.5)
    return values[table]


def draw_first_moment(key, part):
    table = placement_table(key)
    value_key = jax.random.fold_in(key, 22)
    values = jax.random.normal(value_key, (EXPERTS, HID, D), jnp.float32) * 0.3
    return values[table].astype(jnp.bfloat16)


def draw_second_moment(key, part):
    table = placement_table(key)
    value_key = jax.random.fold_in(key, 23)
    values = jnp.exp(jax.random.uniform(value_key, (EXPERTS, HID, D), jnp.float32, -2.3, 1.4))
    return values[table].astype(jnp.bfloat16)


def plant(entries, rng, least, high):
    longest = entries.shape.index(max(entries.shape))
    spots = []
    for shift in (0, 1):
        where = [jax.random.randint(jax.random.fold_in(rng, axis), (), 0, length) for axis, length in enumerate(entries.shape)]
        where[longest] = (where[longest] + shift) % entries.shape[longest]
        spots.append(tuple(where))
    return entries.at[spots[0]].set(least).at[spots[1]].set(high)


def levels(key, dims, split, low, largest):
    def one(axis_at, parts):
        draws = jax.random.uniform(jax.random.fold_in(jax.random.fold_in(key, 6), axis_at), (parts,), jnp.float32, low / len(split), largest / len(split))
        return jnp.repeat(jnp.exp(draws), dims[axis_at] // parts).reshape((-1,) + (1,) * (len(dims) - axis_at - 1))

    factor_of = one(*split[0])
    for cut in split[1:]:
        factor_of = factor_of * one(*cut)
    return factor_of


def shared_out(key, own, number, rows, number_of, top, bound, slope):
    sequence = jax.random.permutation(key, number_of)
    packed, usual = portions_of(number_of, rows * top, bound, slope, True), portions_of(number_of, rows * top, bound, slope, False)
    places = jnp.arange(number_of)

    def named(sizes, turn):
        used = int((sizes > 0).sum())
        fixed = max(1, used // 4)
        passed = fixed + (places - fixed + turn * (used - fixed)) % max(1, number_of - fixed)
        return jnp.zeros((number_of,), jnp.int32).at[sequence[jnp.where(places < fixed, places, passed)]].set(jnp.asarray(sizes, jnp.int32))

    sizes = jnp.where(number % 4 == 0, named(packed, number // 4), named(usual, number - number // 4 - 1))
    mixed = jax.random.permutation(jax.random.fold_in(own, 3), number_of)
    donor, receiver = mixed[0:number_of // 2 * 2:2], mixed[1:number_of // 2 * 2:2]
    margin = jnp.minimum(sizes[donor] - 1, bound - sizes[receiver]) // 2
    margin = jnp.where((donor == sequence[0]) | (receiver == sequence[0]) | (sizes[receiver] == 0), 0, jnp.maximum(margin, 0))
    passed = jax.random.randint(jax.random.fold_in(own, 4), (number_of // 2,), 0, 1 << 20) % (margin + 1)
    sizes = sizes.at[donor].add(-passed).at[receiver].add(passed)
    members = jnp.searchsorted(jnp.cumsum(sizes), jnp.arange(rows * top), side="right").astype(jnp.int32)
    table = members.reshape(top, rows).T
    table = table[jax.random.permutation(jax.random.fold_in(own, 1), rows)]
    turn = jax.random.randint(jax.random.fold_in(own, 2), (rows, 1), 0, top)
    return jnp.take_along_axis(table, (jnp.arange(top)[None, :] + turn) % top, axis=1)


def portions_of(number_of, total, bound, lean, full):
    weights = [(1 << 20) // math.isqrt(standing ** lean) + 1 for standing in range(1, number_of + 1)]
    largest = bound if full else min(bound, max(-(-total // number_of), total * weights[0] // sum(weights)))
    least = 1 if total - largest >= number_of - 1 else 0
    given, spare = [largest] + [least] * (number_of - 1), total - largest - least * (number_of - 1)
    while spare > 0:
        candidates = [i for i in range(1, number_of) if given[i] < largest] or [i for i in range(1, number_of) if given[i] < bound]
        pool, budget = sum([weights[i] for i in candidates]), spare
        for i in candidates:
            more = min(bound - given[i], max(1, budget * weights[i] // pool), spare)
            given[i] = given[i] + more
            spare = spare - more
    return np.array(given)


def gaussian(stream_key, extent, spread, reach, pieces=(), held_as=jnp.bfloat16):
    array = jax.random.normal(stream_key, extent, jnp.float32) * spread
    if len(pieces) > 0:
        array = levels(stream_key, extent, pieces, -0.22, 0.18) * array
    return jnp.clip(array, min=-reach, max=reach).astype(held_as)


def setup_inputs(seed: int = 0) -> dict:
    arg_keys = jax.random.split(jax.random.key(seed), 10)
    grad_out = gaussian(arg_keys[0], (TOKENS, D), 0.25, 1.5, ((0, 256),))
    gate_probs = jnp.clip(0.05 + 0.25 * jax.random.uniform(arg_keys[1], (TOKENS, TOPK), jnp.float32) ** levels(arg_keys[1], (TOKENS, TOPK), ((0, 256),), -0.2, 0.2), 0.05, 0.3)
    expert_route_keys = jax.random.split(jax.random.fold_in(arg_keys[2], 1), TOKENS // TOK_DEV)
    expert_route_turns = jax.random.permutation(jax.random.fold_in(arg_keys[2], 3), TOKENS // TOK_DEV)
    expert_route = jax.vmap(lambda own, number: shared_out(jax.random.fold_in(arg_keys[2], 2), own, number, TOK_DEV, EXPERTS, TOPK, CAP, 1))(expert_route_keys, expert_route_turns).reshape((TOKENS, TOPK))
    replica_pick = plant(jax.random.randint(arg_keys[3], (TOKENS, TOPK), 0, 60), jax.random.fold_in(arg_keys[3], 1), 0, 59).astype(jnp.int32)
    slot_expert = draw_slot_expert(jax.random.fold_in(arg_keys[9], 71), 0)
    saved_hidden = gaussian(arg_keys[5], (N_DP, N_EXPERT, N_EXPERT, SLOT_DEV, CAP, HID), 1.0, 6.0, ((0, 8), (1, 32)))
    master = draw_master(jax.random.fold_in(arg_keys[9], 71), 0)
    first_moment = draw_first_moment(jax.random.fold_in(arg_keys[9], 71), 0)
    second_moment = draw_second_moment(jax.random.fold_in(arg_keys[9], 71), 0)
    return {"grad_out": grad_out, "gate_probs": gate_probs, "expert_route": expert_route, "replica_pick": replica_pick, "slot_expert": slot_expert, "saved_hidden": saved_hidden, "master": master, "first_moment": first_moment, "second_moment": second_moment}


beta_one = 0.9
beta_two = 0.95
learn_rate = 0.00022
decay_rate = 0.1
epsilon = 1e-08
correct_one = 0.6513215599
correct_two = 0.4012630607

def reference(grad_out, gate_probs, expert_route, replica_pick, slot_expert, saved_hidden, master, first_moment, second_moment):
    dp_count, dev_count, _, slot_dev, capacity, hidden_count = saved_hidden.shape
    slot_count = slot_expert.shape[0]
    feature_count = grad_out.shape[1]
    top_count = gate_probs.shape[1]
    tok_rows = grad_out.shape[0] // (dp_count * dev_count)
    assigned = tok_rows * top_count
    slot_ids = jnp.arange(slot_count, dtype=jnp.int32)
    same_expert = slot_expert[:, None] == slot_expert[None, :]
    slot_rank = lax.optimization_barrier(jnp.sum(same_expert & (slot_ids[None, :] < slot_ids[:, None]), axis=1)).astype(jnp.int32)
    experts = expert_route.reshape(dp_count, dev_count, assigned)
    replica_picks = replica_pick.reshape(dp_count, dev_count, assigned)
    host_mask = slot_expert[None, None, None, :] == experts[..., None]
    copy_count = lax.optimization_barrier(jnp.sum(host_mask.astype(jnp.int32), axis=-1)).astype(jnp.int32)
    chosen = host_mask & (slot_rank[None, None, None, :] == (replica_picks % copy_count)[..., None])
    target = lax.optimization_barrier(jnp.sum(jnp.where(chosen, slot_ids, 0), axis=-1)).astype(jnp.int32)
    onehot = (target[..., None] == slot_ids).astype(jnp.int32)
    before = jnp.cumsum(onehot, axis=2) - onehot
    position = lax.optimization_barrier(jnp.sum(onehot * before, axis=-1)).astype(jnp.int32)
    dp_grid = jnp.broadcast_to(jnp.arange(dp_count, dtype=jnp.int32)[:, None, None], target.shape)
    dev_grid = jnp.broadcast_to(jnp.arange(dev_count, dtype=jnp.int32)[None, :, None], target.shape)
    row_grid = jnp.broadcast_to(jnp.arange(assigned, dtype=jnp.int32)[None, None, :], target.shape)
    lookup = jnp.full((dp_count, slot_count, dev_count, capacity), -1, jnp.int32)
    lookup = lookup.at[dp_grid, target, dev_grid, position].set(row_grid)
    token_grads = grad_out.reshape(dp_count, dev_count, tok_rows, feature_count)
    gate_values = gate_probs.astype(jnp.bfloat16).reshape(dp_count, dev_count, assigned)
    dp_index = jnp.arange(dp_count, dtype=jnp.int32)[:, None, None]
    dev_index = jnp.arange(dev_count, dtype=jnp.int32)[None, :, None]

    def per_slot(slot_id):
        row_ids = lax.dynamic_index_in_dim(lookup, slot_id, axis=1, keepdims=False)
        live_rows = row_ids >= 0
        safe_rows = jnp.maximum(row_ids, 0)
        picked = token_grads[dp_index, dev_index, safe_rows // top_count]
        bf_zero = jnp.zeros((), jnp.bfloat16)
        dispatched = jnp.where(live_rows[..., None], picked, bf_zero)
        gate_rows = jnp.where(live_rows, gate_values[dp_index, dev_index, safe_rows], bf_zero)
        device_part = lax.dynamic_index_in_dim(saved_hidden, slot_id // slot_dev, axis=1, keepdims=False)
        hidden = lax.dynamic_index_in_dim(device_part, slot_id % slot_dev, axis=2, keepdims=False)
        weight = lax.dynamic_index_in_dim(master, slot_id, axis=0, keepdims=False).astype(jnp.bfloat16)
        projected = jnp.einsum('pqcd,hd->pqch', dispatched.astype(jnp.float32), weight.astype(jnp.float32))
        gate_scale = gate_rows.astype(jnp.float32)[..., None]
        hidden_grad = (gate_scale * projected).astype(jnp.bfloat16)
        gate_terms = lax.optimization_barrier(jnp.sum(hidden.astype(jnp.float32) * projected, axis=-1))
        scaled = (gate_scale * dispatched.astype(jnp.float32)).astype(jnp.bfloat16)
        partial_value = jnp.einsum('pqch,pqcd->phd', hidden.astype(jnp.float32), scaled.astype(jnp.float32))
        rounded = lax.optimization_barrier(partial_value.astype(jnp.bfloat16))
        summed = lax.optimization_barrier(jnp.sum(rounded.astype(jnp.float32), axis=0))
        return (hidden_grad, gate_terms, summed)
    hidden_all, gate_all, grad_all = lax.map(per_slot, slot_ids)
    expert_sums = jax.ops.segment_sum(grad_all, slot_expert, num_segments=slot_count)
    grad_total = expert_sums[slot_expert]
    new_first = beta_one * first_moment.astype(jnp.float32) + (1.0 - beta_one) * grad_total
    new_second = beta_two * second_moment.astype(jnp.float32) + (1.0 - beta_two) * grad_total * grad_total
    update = new_first / correct_one / (jnp.sqrt(new_second / correct_two) + epsilon) + decay_rate * master
    new_master = master - learn_rate * update
    hidden_grad = hidden_all.reshape(dev_count, slot_dev, dp_count, dev_count, capacity, hidden_count)
    hidden_grad = hidden_grad.transpose(2, 0, 3, 1, 4, 5)
    gate_grad = gate_all[target, dp_grid, dev_grid, position].reshape(dp_count * dev_count * tok_rows, top_count)
    return (hidden_grad, gate_grad, new_master, new_first.astype(jnp.bfloat16), new_second.astype(jnp.bfloat16))
```

```python
import jax
import jax.numpy as jnp
from jax import lax
from jax.sharding import PartitionSpec as P

beta_one = 0.9
beta_two = 0.95
learn_rate = 0.00022
decay_rate = 0.1
epsilon = 1e-08
correct_one = 0.6513215599
correct_two = 0.4012630607


def on_device(
    grad_out,
    gate_probs,
    expert_route,
    replica_pick,
    slot_expert,
    saved_hidden,
    master,
    first_moment,
    second_moment,
):
    slots = slot_expert.shape[0]
    cap = saved_hidden.shape[4]
    feats = grad_out.shape[1]
    toks, top = gate_probs.shape
    rows_own = master.shape[1]
    weights = lax.optimization_barrier(master[0].astype(jnp.bfloat16))
    gathered = lax.all_gather(weights, "dp", axis=0, tiled=True)
    ids = jnp.arange(slots, dtype=jnp.int32)
    same = slot_expert[:, None] == slot_expert[None, :]
    rank = jnp.sum(same & (ids[None, :] < ids[:, None]), axis=1)
    route = expert_route.T[:, None, :]
    pick = replica_pick.T
    host = slot_expert[None, :, None] == route
    copies = jnp.sum(host.astype(jnp.int32), axis=1)
    chosen = host & (rank[None, :, None] == (pick % copies)[:, None, :])
    taken = jnp.any(chosen, axis=0)
    order = jnp.arange(toks, dtype=jnp.int32)
    before = (order[:, None] < order[None, :]).astype(jnp.bfloat16)
    place = jnp.dot(taken.astype(jnp.bfloat16), before, preferred_element_type=jnp.float32)
    gate_of = jnp.sum(
        jnp.where(chosen, gate_probs.T.astype(jnp.bfloat16).astype(jnp.float32)[:, None, :], 0.0), axis=0
    )
    spot = jnp.where(taken, place.astype(jnp.int32), -1)
    hot = spot[:, None, :] == jnp.arange(cap, dtype=jnp.int32)[None, :, None]
    send_gates = jnp.sum(jnp.where(hot, gate_of[:, None, :], 0.0), axis=2).astype(jnp.bfloat16)
    send_rows = jnp.dot(
        hot.astype(jnp.bfloat16).reshape(slots * cap, toks), grad_out, preferred_element_type=jnp.float32
    ).astype(jnp.bfloat16)
    rows = lax.all_to_all(
        send_rows.reshape(slots, cap, feats), "expert", split_axis=0, concat_axis=0, tiled=True
    ).reshape(slots * cap, feats)
    gates = lax.all_to_all(send_gates, "expert", split_axis=0, concat_axis=0, tiled=True)
    scale = gates.astype(jnp.float32).reshape(slots * cap, 1)
    hidden = saved_hidden.reshape(slots * cap, -1)
    gated = (hidden.astype(jnp.float32) * scale).astype(jnp.bfloat16)
    partial = lax.dot_general(
        gated, rows, (((0,), (0,)), ((), ())), preferred_element_type=jnp.float32
    ).astype(jnp.bfloat16)
    reduced = lax.psum_scatter(partial, "dp", scatter_dimension=0, tiled=True)
    projected = lax.dot_general(rows, gathered, (((1,), (1,)), ((), ())), preferred_element_type=jnp.float32)
    hidden_grad = (scale * projected).astype(jnp.bfloat16).reshape(saved_hidden.shape)
    terms = jnp.sum(hidden.astype(jnp.float32) * projected, axis=-1).reshape(slots, cap)
    returned = lax.all_to_all(terms, "expert", split_axis=0, concat_axis=0, tiled=True)
    by_token = jnp.sum(jnp.where(hot, returned[:, :, None], 0.0), axis=1)
    gate_grad = jnp.sum(jnp.where(chosen, by_token[None], 0.0), axis=1).T
    part = rows_own // slots
    shards = lax.all_to_all(
        reduced.reshape(slots, part, feats), "expert", split_axis=0, concat_axis=0, tiled=True
    )
    summed = lax.dot_general(
        same.astype(jnp.bfloat16),
        shards,
        (((1,), (0,)), ((), ())),
        preferred_element_type=jnp.float32,
    ).astype(jnp.bfloat16)
    back = lax.all_to_all(summed, "expert", split_axis=0, concat_axis=0, tiled=True)
    total = back.reshape(1, rows_own, feats).astype(jnp.float32)
    new_first = beta_one * first_moment.astype(jnp.float32) + (1.0 - beta_one) * total
    new_second = beta_two * second_moment.astype(jnp.float32) + (1.0 - beta_two) * total * total
    update = (
        new_first / correct_one / (jnp.sqrt(new_second / correct_two) + epsilon) + decay_rate * master
    )
    new_master = master - learn_rate * update
    return (
        hidden_grad,
        gate_grad,
        new_master,
        new_first.astype(jnp.bfloat16),
        new_second.astype(jnp.bfloat16),
    )


def solution(mesh):
    tokens = P(("dp", "expert"), None)
    acts = P("dp", "expert", None, None, None, None)
    shard = P("expert", "dp", None)
    return jax.shard_map(
        on_device,
        mesh=mesh,
        in_specs=(tokens, tokens, tokens, tokens, P(), acts, shard, shard, shard),
        out_specs=(acts, tokens, shard, shard, shard),
        check_vma=False,
    )
```

```python
import functools

import jax
import jax.numpy as jnp
from jax import lax
from jax.experimental import pallas as pl
from jax.experimental.pallas import tpu as pltpu
from jax.sharding import PartitionSpec as P

HOT = 3
CORES = 2
BF = jnp.bfloat16
F32 = jnp.float32
MESH = pl.DeviceIdType.MESH

beta_one = 0.9
beta_two = 0.95
learn_rate = 0.00022
decay_rate = 0.1
epsilon = 1e-08
correct_one = 0.6513215599
correct_two = 0.4012630607


def kernel(
    nx,
    ny,
    nz,
    chunks,
    cap,
    meta,
    share,
    tok,
    hid,
    mas,
    fst,
    snd,
    hg,
    back,
    nm,
    nf,
    ns,
    xg,
    wg,
    sendy,
    rows,
    pick2,
    gcol,
    gated,
    proj,
    csend,
    crecv,
    ownh,
    xsend,
    xrecv,
    xown,
    gsh,
    hs1,
    hr1,
    ts,
    tr,
    hs2,
    hr2,
    mz,
    rel,
    relr,
    ret,
    retr,
    bz,
    bk,
    load_sem,
    zs,
    zr,
    ys,
    yr,
    wxs,
    wxr,
    wcs,
    wcr,
    cs,
    cr,
    xs,
    xr,
    h1s,
    h1r,
    tss,
    tsr,
    h2s,
    h2r,
    ms,
    mr,
    rs,
    rr,
    qs,
    qr,
    bs,
    br,
):
    p, q = lax.axis_index("dp"), lax.axis_index("expert")
    x, c = p // CORES, lax.rem(p, CORES)
    z, y = q // ny, lax.rem(q, ny)
    toks = xg.shape[2]
    dk = xg.shape[3]
    shard = wg.shape[3]
    far, near = nz // 2, nz - 1 - nz // 2
    block = nz * cap
    pair = 2 * cap
    part = shard // nz

    def at_x(j):
        return lax.rem(x + j + nx, nx)

    def at_y(j):
        return lax.rem(y + j + ny, ny)

    def at_z(j):
        return lax.rem(z + j + nz, nz)

    def remote(src, dst, ssem, rsem, pp, qq):
        return pltpu.make_async_remote_copy(
            src_ref=src, dst_ref=dst, send_sem=ssem, recv_sem=rsem, device_id=(pp, qq), device_id_type=MESH
        )

    def lanes(k):
        return pl.ds(pl.multiple_of(k * dk, 128), dk)

    def load(k):
        return pltpu.make_async_copy(tok.at[:, lanes(k)], xg.at[k, z], load_sem.at[k])

    for k in range(chunks):
        load(k).start()

    barrier = pltpu.get_barrier_semaphore()
    peers = [(p, at_z(j) * ny + y) for j in range(1, nz)]
    peers += [(p, z * ny + at_y(j)) for j in range(1, ny)]
    peers += [(at_x(j) * CORES + c, q) for j in range(1, nx)]
    other = x * CORES + 1 - c
    peers += [(other, q)]
    for peer in peers:
        pl.semaphore_signal(barrier, inc=1, device_id=peer, device_id_type=MESH)
    pl.semaphore_wait(barrier, len(peers))

    def meta_copy(j):
        return remote(meta.at[at_z(j)], mz.at[z], ms.at[j - 1], mr.at[j - 1], p, at_z(j) * ny + y)

    def rel_copy(j):
        return remote(rel.at[at_y(j)], relr.at[y], rs.at[j - 1], rr.at[j - 1], p, z * ny + at_y(j))

    def ret_copy(j):
        return remote(ret.at[at_y(j)], retr.at[y], qs.at[j - 1], qr.at[j - 1], p, z * ny + at_y(j))

    def back_copy(j):
        return remote(bz.at[at_z(j)], bk.at[z], bs.at[j - 1], br.at[j - 1], p, at_z(j) * ny + y)

    def hop(d, h, k):
        sign = 1 - 2 * d
        origin = lax.rem(z - sign * (h - 1) + nz, nz)
        to = lax.rem(z + sign + nz, nz)
        return remote(
            xg.at[k, origin], xg.at[k, origin], zs.at[d, h - 1, k], zr.at[d, h - 1, k], p, to * ny + y
        )

    def hops(h, k):
        if h <= near:
            return [hop(0, h, k), hop(1, h, k)]
        if h <= far:
            return [hop(lax.rem(k, 2), h, k)]
        return []

    def weight_copy(j, k):
        return remote(
            wg.at[k, c, x], wg.at[k, c, x], wxs.at[j - 1, k], wxr.at[j - 1, k], at_x(j) * CORES + c, q
        )

    def weight_pass(k):
        return remote(wg.at[k, c], wg.at[k, c], wcs.at[k], wcr.at[k], other, q)

    def row_copy(j, k):
        return remote(
            sendy.at[lax.rem(k, 2), at_y(j)],
            rows.at[k, y],
            ys.at[j - 1, k],
            yr.at[j - 1, k],
            p,
            z * ny + at_y(j),
        )

    def core_copy(k):
        return remote(csend.at[lax.rem(k, 2)], crecv.at[k], cs.at[k], cr.at[k], other, q)

    def x_copy(j, k):
        return remote(
            xsend.at[lax.rem(k, 2), at_x(j)],
            xrecv.at[k, x],
            xs.at[j - 1, k],
            xr.at[j - 1, k],
            at_x(j) * CORES + c,
            q,
        )

    def first_copy(j, k):
        return remote(
            hs1.at[k, at_z(j)], hr1.at[k, z], h1s.at[j - 1, k], h1r.at[j - 1, k], p, at_z(j) * ny + y
        )

    def table_copy(j, k):
        return remote(ts.at[k], tr.at[k, y], tss.at[j - 1, k], tsr.at[j - 1, k], p, z * ny + at_y(j))

    def second_copy(j, k):
        return remote(
            hs2.at[k, at_z(j)], hr2.at[k, z], h2s.at[j - 1, k], h2r.at[j - 1, k], p, at_z(j) * ny + y
        )

    def when(k):
        return pl.when((k >= 0) & (k < chunks))

    for j in range(1, nz):
        meta_copy(j).start()
    mz[z] = meta[z]
    proj[...] = jnp.zeros_like(proj)

    spot_row = lax.broadcasted_iota(jnp.int32, (cap, toks), 0).astype(F32)

    def step(tau, carry):
        for h in range(far, 0, -1):

            @when(tau - h)
            def _(h=h, k=tau - h):
                for copy in hops(h, k):
                    copy.wait()
                for copy in hops(h + 1, k):
                    copy.start()

        @when(tau)
        def _(k=tau):
            load(k).wait()
            for copy in hops(1, k):
                copy.start()
            wg[k, c, x] = mas[:, lanes(k)].astype(BF)
            for j in range(1, nx):
                weight_copy(j, k).start()

        @when(tau - 2)
        def _(k=tau - 2):
            for j in range(1, nx):
                weight_copy(j, k).wait()
            weight_pass(k).start()

        @pl.when(tau == 1)
        def _():
            for j in range(1, nz):
                meta_copy(j).wait()
            for yy in range(ny):
                for zz in range(nz):
                    rel[yy, zz : zz + 1, :] = mz[zz, yy : yy + 1, :]
                    rel[yy, nz + zz : nz + zz + 1, :] = mz[zz, ny + yy : ny + yy + 1, :]
            for j in range(1, ny):
                rel_copy(j).start()
            relr[y] = rel[y]
            zero = jnp.zeros((cap, toks), F32)
            for jj in range(nz // 2):
                for yy in range(ny):
                    one = [
                        jnp.where(mz[2 * jj + i, yy : yy + 1, :] == spot_row, 1.0, 0.0) for i in (0, 1)
                    ]
                    top = jnp.concatenate([one[0], zero], axis=1)
                    low = jnp.concatenate([zero, one[1]], axis=1)
                    pick2[jj, yy * pair : (yy + 1) * pair, :] = jnp.concatenate([top, low], axis=0).astype(BF)

        @pl.when(tau == 2)
        def _():
            for j in range(1, ny):
                rel_copy(j).wait()
            for yy in range(ny):
                for zz in range(nz):
                    hit = relr[yy, zz : zz + 1, :] == spot_row
                    gate = jnp.where(hit, relr[yy, nz + zz : nz + zz + 1, :], 0.0)
                    column = jnp.sum(gate, axis=1, keepdims=True)
                    start = yy * block + zz * cap
                    gcol[start : start + cap, :] = jnp.broadcast_to(column, (cap, 128))

            def turn(i, carry):
                here = pl.ds(pl.multiple_of(i * 128, 128), 128)
                scaled = hid[here, :].astype(F32) * gcol[here, :][:, 0:1]
                gated[:, here] = scaled.T.astype(BF)
                return carry

            lax.fori_loop(0, hid.shape[0] // 128, turn, 0)

        @when(tau - far)
        def _(k=tau - far):
            slot = lax.rem(k, 2)

            def choose(jj, carry):
                two = xg[k, pl.ds(2 * jj, 2)].reshape(2 * toks, dk)
                got = jnp.dot(pick2[jj], two, preferred_element_type=F32).astype(BF)
                here = pl.ds(pl.multiple_of(jj * pair, pair), pair)
                for yy in range(ny):
                    sendy[slot, yy, here, :] = got[yy * pair : (yy + 1) * pair, :]
                return carry

            lax.fori_loop(0, nz // 2, choose, 0)
            for j in range(1, ny):
                row_copy(j, k).start()
            rows[k, y] = sendy[slot, y]

        @when(tau - far - 6)
        def _(k=tau - far - 6):
            for j in range(1, nz):
                second_copy(j, k).wait()
            flag = share[0, q]
            for e in range(1, HOT):
                flag = flag + share[e, q]

            def adam(b, carry):
                here = pl.ds(pl.multiple_of(b * part, part), part)
                grad = flag * hr2[k, b].astype(F32) + (1.0 - flag) * gsh[k, here, :]
                old = mas[here, lanes(k)]
                first = beta_one * fst[here, lanes(k)].astype(F32) + (1.0 - beta_one) * grad
                second = beta_two * snd[here, lanes(k)].astype(F32) + (1.0 - beta_two) * grad * grad
                update = first / correct_one / (jnp.sqrt(second / correct_two) + epsilon) + decay_rate * old
                nm[here, lanes(k)] = old - learn_rate * update
                nf[here, lanes(k)] = first.astype(BF)
                ns[here, lanes(k)] = second.astype(BF)
                return carry

            lax.fori_loop(0, nz, adam, 0)

        @when(tau - far - 5)
        def _(k=tau - far - 5):
            for j in range(1, ny):
                table_copy(j, k).wait()
            total = []
            for e in range(HOT):
                acc = tr[k, 0, e].astype(F32)
                for yy in range(1, ny):
                    acc = acc + tr[k, yy, e].astype(F32)
                total.append(acc)
            for zz in range(nz):
                acc = share[0, zz * ny + y] * total[0]
                for e in range(1, HOT):
                    acc = acc + share[e, zz * ny + y] * total[e]
                hs2[k, zz] = acc.astype(BF)
            for j in range(1, nz):
                second_copy(j, k).start()
            hr2[k, z] = hs2[k, z]

        @when(tau - far - 4)
        def _(k=tau - far - 4):
            for j in range(1, nz):
                first_copy(j, k).wait()
            sums = [jnp.zeros((part, dk), F32)] * HOT
            for zz in range(nz):
                value = hr1[k, zz].astype(F32)
                sums = [sums[e] + share[e, zz * ny + y] * value for e in range(HOT)]
            for e in range(HOT):
                ts[k, e] = sums[e].astype(BF)
            for j in range(1, ny):
                table_copy(j, k).start()
            tr[k, y] = ts[k]

        @when(tau - far - 3)
        def _(k=tau - far - 3):
            for j in range(1, nx):
                x_copy(j, k).wait()

            def add(b, carry):
                here = pl.ds(pl.multiple_of(b * part, part), part)
                value = xown[here, :]
                for j in range(1, nx):
                    value = value + xrecv[k, at_x(-j), here, :].astype(F32)
                gsh[k, here, :] = value
                hs1[k, b] = value.astype(BF)
                return carry

            lax.fori_loop(0, nz, add, 0)
            for j in range(1, nz):
                first_copy(j, k).start()
            hr1[k, z] = hs1[k, z]

        @when(tau - far - 2)
        def _(k=tau - far - 2):
            core_copy(k).wait()
            for j in range(1, nx):
                xsend[lax.rem(k, 2), at_x(j)] = (ownh[at_x(j)] + crecv[k, at_x(j)].astype(F32)).astype(BF)
                x_copy(j, k).start()
            xown[...] = ownh[x] + crecv[k, x].astype(F32)

        @when(tau - far - 1)
        def _(k=tau - far - 1):
            for j in range(1, ny):
                row_copy(j, k).wait()
            slot = lax.rem(k, 2)

            def half(xx, core):
                here = pl.ds(pl.multiple_of((xx * CORES + core) * shard, shard), shard)
                return jnp.dot(
                    gated[here, :], rows[k].reshape(ny * block, dk), preferred_element_type=F32
                )

            def theirs(xx, carry):
                csend[slot, xx] = half(xx, 1 - c).astype(BF)
                return carry

            def mine(xx, carry):
                ownh[xx] = half(xx, c)
                return carry

            def project(xx, carry):
                w = jnp.concatenate([wg[k, 0, xx], wg[k, 1, xx]], axis=0)
                here = pl.ds(pl.multiple_of(xx * CORES * shard, CORES * shard), CORES * shard)
                proj[:, here] += lax.dot_general(
                    rows[k].reshape(ny * block, dk), w, (((1,), (1,)), ((), ())), preferred_element_type=F32
                )
                return carry

            lax.fori_loop(0, nx, theirs, 0)
            core_copy(k).start()
            lax.fori_loop(0, nx, mine, 0)
            weight_pass(k).wait()
            lax.fori_loop(0, nx, project, 0)

        @pl.when(tau == chunks + far + 1)
        def _():
            def finish(i, carry):
                yy, jj = i // (nz // 2), lax.rem(i, nz // 2)
                here = pl.ds(pl.multiple_of(i * pair, pair), pair)
                value = proj[here, :]
                hg[here, :] = (gcol[here, :][:, 0:1] * value).astype(BF)
                term = jnp.sum(hid[here, :].astype(F32) * value, axis=1, keepdims=True)
                for half_of in (0, 1):
                    zz = 2 * jj + half_of
                    hit = relr[yy, pl.ds(zz, 1), :] == spot_row
                    piece = term[half_of * cap : (half_of + 1) * cap, :]
                    ret[yy, pl.ds(zz, 1), :] = jnp.sum(jnp.where(hit, piece, 0.0), axis=0, keepdims=True)
                return carry

            lax.fori_loop(0, ny * nz // 2, finish, 0)
            for j in range(1, ny):
                ret_copy(j).start()
            retr[y] = ret[y]

        @pl.when(tau == chunks + far + 2)
        def _():
            for j in range(1, ny):
                ret_copy(j).wait()
            bz[...] = jnp.zeros_like(bz)
            for zz in range(nz):
                for yy in range(ny):
                    bz[zz, yy : yy + 1, :] = retr[yy, zz : zz + 1, :]
            for j in range(1, nz):
                back_copy(j).start()

        @pl.when(tau == chunks + far + 3)
        def _():
            for j in range(1, nz):
                back_copy(j).wait()
            bk[z] = bz[z]
            back[...] = bk[...]

        return carry

    lax.fori_loop(0, chunks + far + 6, step, 0)


def whole(nx, ny, nz, chunks, meta, share, tok, hid, mas, fst, snd, cap):
    toks, feats = tok.shape
    dk = feats // chunks
    shard = mas.shape[0]
    units = hid.shape[1]
    count = hid.shape[0]
    block = nz * cap
    part = shard // nz
    vmem = pl.BlockSpec(memory_space=pltpu.VMEM)
    dma = pltpu.SemaphoreType.DMA
    n_dma = lambda *s: dma(tuple(max(1, v) for v in s))
    scratch = [
        pltpu.VMEM((chunks, nz, toks, dk), BF),
        pltpu.VMEM((chunks, CORES, nx, shard, dk), BF),
        pltpu.VMEM((2, ny, block, dk), BF),
        pltpu.VMEM((chunks, ny, block, dk), BF),
        pltpu.VMEM((nz // 2, ny * 2 * cap, 2 * toks), BF),
        pltpu.VMEM((count, 128), F32),
        pltpu.VMEM((units, count), BF),
        pltpu.VMEM((count, units), F32),
        pltpu.VMEM((2, nx, shard, dk), BF),
        pltpu.VMEM((chunks, nx, shard, dk), BF),
        pltpu.VMEM((nx, shard, dk), F32),
        pltpu.VMEM((2, nx, shard, dk), BF),
        pltpu.VMEM((chunks, nx, shard, dk), BF),
        pltpu.VMEM((shard, dk), F32),
        pltpu.VMEM((chunks, shard, dk), F32),
        pltpu.VMEM((chunks, nz, part, dk), BF),
        pltpu.VMEM((chunks, nz, part, dk), BF),
        pltpu.VMEM((chunks, HOT, part, dk), BF),
        pltpu.VMEM((chunks, ny, HOT, part, dk), BF),
        pltpu.VMEM((chunks, nz, part, dk), BF),
        pltpu.VMEM((chunks, nz, part, dk), BF),
        pltpu.VMEM((nz, 8, 128), F32),
        pltpu.VMEM((ny, 2 * nz, 128), F32),
        pltpu.VMEM((ny, 2 * nz, 128), F32),
        pltpu.VMEM((ny, nz, 128), F32),
        pltpu.VMEM((ny, nz, 128), F32),
        pltpu.VMEM((nz, 8, 128), F32),
        pltpu.VMEM((nz, 8, 128), F32),
        n_dma(chunks),
        n_dma(2, nz // 2, chunks),
        n_dma(2, nz // 2, chunks),
        n_dma(ny - 1, chunks),
        n_dma(ny - 1, chunks),
        n_dma(nx - 1, chunks),
        n_dma(nx - 1, chunks),
        n_dma(chunks),
        n_dma(chunks),
        n_dma(chunks),
        n_dma(chunks),
        n_dma(nx - 1, chunks),
        n_dma(nx - 1, chunks),
        n_dma(nz - 1, chunks),
        n_dma(nz - 1, chunks),
        n_dma(ny - 1, chunks),
        n_dma(ny - 1, chunks),
        n_dma(nz - 1, chunks),
        n_dma(nz - 1, chunks),
        n_dma(nz - 1),
        n_dma(nz - 1),
        n_dma(ny - 1),
        n_dma(ny - 1),
        n_dma(ny - 1),
        n_dma(ny - 1),
        n_dma(nz - 1),
        n_dma(nz - 1),
    ]
    return pl.pallas_call(
        functools.partial(kernel, nx, ny, nz, chunks, cap),
        out_shape=(
            jax.ShapeDtypeStruct((count, units), BF),
            jax.ShapeDtypeStruct((nz, 8, 128), F32),
            jax.ShapeDtypeStruct((shard, feats), F32),
            jax.ShapeDtypeStruct((shard, feats), BF),
            jax.ShapeDtypeStruct((shard, feats), BF),
        ),
        in_specs=[
            vmem,
            pl.BlockSpec(memory_space=pltpu.SMEM),
            pl.BlockSpec(memory_space=pl.ANY),
            vmem,
            vmem,
            vmem,
            vmem,
        ],
        out_specs=(vmem,) * 5,
        scratch_shapes=scratch,
        compiler_params=pltpu.CompilerParams(
            collective_id=0, has_side_effects=True, vmem_limit_bytes=62 * 2**20
        ),
        cost_estimate=pl.CostEstimate(
            flops=4 * count * units * feats, bytes_accessed=20 * 2**20, transcendentals=0
        ),
    )(meta, share, tok, hid, mas, fst, snd)


def on_device(
    nx,
    ny,
    nz,
    chunks,
    grad_out,
    gate_probs,
    expert_route,
    replica_pick,
    slot_expert,
    saved_hidden,
    master,
    first_moment,
    second_moment,
):
    slots = slot_expert.shape[0]
    cap = saved_hidden.shape[4]
    units = saved_hidden.shape[5]
    toks, top = gate_probs.shape
    ids = jnp.arange(slots, dtype=jnp.int32)
    same = slot_expert[:, None] == slot_expert[None, :]
    rank = jnp.sum(same & (ids[None, :] < ids[:, None]), axis=1)
    host = slot_expert[None, :, None] == expert_route.T[:, None, :]
    copies = jnp.sum(host.astype(jnp.int32), axis=1)
    chosen = host & (rank[None, :, None] == (replica_pick.T % copies)[:, None, :])
    taken = jnp.any(chosen, axis=0)
    order = jnp.arange(toks, dtype=jnp.int32)
    before = (order[:, None] < order[None, :]).astype(BF)
    place = jnp.dot(taken.astype(BF), before, preferred_element_type=F32)
    spot = jnp.where(taken, place, -1.0)
    gates = gate_probs.T.astype(BF).astype(F32)
    gate_of = jnp.sum(jnp.where(chosen, gates[:, None, :], 0.0), axis=0)
    meta = jnp.concatenate([spot.reshape(nz, ny, toks), gate_of.reshape(nz, ny, toks)], axis=1)
    if 2 * ny < 8:
        meta = jnp.pad(meta, ((0, 0), (0, 8 - 2 * ny), (0, 0)))
    share = (slot_expert[None, :] == jnp.arange(HOT, dtype=jnp.int32)[:, None]).astype(F32)
    hidden = saved_hidden.reshape(nz, ny, cap, units).transpose(1, 0, 2, 3).reshape(slots * cap, units)
    hidden_grad, back, new_master, new_first, new_second = whole(
        nx, ny, nz, chunks, meta, share, grad_out, hidden, master[0], first_moment[0], second_moment[0], cap
    )
    by_slot = back[:, :ny, :].reshape(slots, toks)
    gate_grad = jnp.sum(jnp.where(chosen, by_slot[None], 0.0), axis=1).T
    hidden_grad = hidden_grad.reshape(ny, nz, cap, units).transpose(1, 0, 2, 3).reshape(saved_hidden.shape)
    return hidden_grad, gate_grad, new_master[None], new_first[None], new_second[None]


def build(mesh, nx, ny, nz, chunks):
    tokens = P(("dp", "expert"), None)
    acts = P("dp", "expert", None, None, None, None)
    shard = P("expert", "dp", None)
    return jax.shard_map(
        functools.partial(on_device, nx, ny, nz, chunks),
        mesh=mesh,
        in_specs=(tokens, tokens, tokens, tokens, P(), acts, shard, shard, shard),
        out_specs=(acts, tokens, shard, shard, shard),
        check_vma=False,
    )


def solution(mesh):
    ny = 4
    return build(mesh, mesh.shape["dp"] // CORES, ny, mesh.shape["expert"] // ny, 7)
```

```python
import functools

import jax
import jax.numpy as jnp
from jax import lax
from jax.experimental import pallas as pl
from jax.experimental.pallas import tpu as pltpu
from jax.sharding import PartitionSpec as P

HOT = 3
CORES = 2
AHEAD = 1
SLACK = 2
BF = jnp.bfloat16
F32 = jnp.float32
MESH = pl.DeviceIdType.MESH

beta_one = 0.9
beta_two = 0.95
learn_rate = 0.00022
decay_rate = 0.1
epsilon = 1e-08
correct_one = 0.6513215599
correct_two = 0.4012630607


def kernel(
    nx,
    ny,
    nz,
    chunks,
    cap,
    holder,
    route,
    pick,
    prob,
    tok,
    hid_in,
    mas_in,
    fst_in,
    snd_in,
    hg_out,
    gg,
    nm_out,
    nf_out,
    ns_out,
    hid,
    mas,
    fst,
    snd,
    hg,
    nm,
    nf,
    ns,
    chosen,
    taken,
    meta,
    xg,
    wg,
    sendy,
    rows,
    pick2,
    gcol,
    gated,
    proj,
    csend,
    crecv,
    ownh,
    xsend,
    xrecv,
    xown,
    gsh,
    hs1,
    hr1,
    ts,
    tr,
    hs2,
    hr2,
    mz,
    rel,
    relr,
    ret,
    retr,
    bz,
    bk,
    load_sem,
    mas_sem,
    in_sem,
    hid_sem,
    out_sem,
    hg_sem,
    zs,
    zr,
    ys,
    yr,
    wxs,
    wxr,
    wcs,
    wcr,
    cs,
    cr,
    xs,
    xr,
    h1s,
    h1r,
    tss,
    tsr,
    h2s,
    h2r,
    ms,
    mr,
    rs,
    rr,
    qs,
    qr,
    bs,
    br,
):
    p, q = lax.axis_index("dp"), lax.axis_index("expert")
    x, c = p // CORES, lax.rem(p, CORES)
    z, y = q // ny, lax.rem(q, ny)
    toks = xg.shape[2]
    dk = xg.shape[3]
    shard = wg.shape[3]
    far, near = nz // 2, nz - 1 - nz // 2
    block = nz * cap
    pair = 2 * cap
    part = shard // nz
    picked = far + AHEAD

    at_x = [lax.rem(x + j, nx) for j in range(nx)]
    at_y = [lax.rem(y + j, ny) for j in range(ny)]
    at_z = [lax.rem(z + j, nz) for j in range(nz)]
    to_x = [v * CORES + c for v in at_x]
    to_y = [z * ny + v for v in at_y]
    to_z = [v * ny + y for v in at_z]
    other = x * CORES + 1 - c

    def remote(src, dst, ssem, rsem, pp, qq):
        return pltpu.make_async_remote_copy(
            src_ref=src, dst_ref=dst, send_sem=ssem, recv_sem=rsem, device_id=(pp, qq), device_id_type=MESH
        )

    def lanes(k):
        return pl.ds(pl.multiple_of(k * dk, 128), dk)

    def load(k):
        return pltpu.make_async_copy(tok.at[:, lanes(k)], xg.at[k, z], load_sem.at[k])

    def load_hid(yy):
        return pltpu.make_async_copy(hid_in.at[:, yy], hid.at[yy], hid_sem.at[yy])

    def save_hg(yy):
        return pltpu.make_async_copy(hg.at[yy], hg_out.at[:, yy], hg_sem.at[yy])

    load_mas = pltpu.make_async_copy(mas_in, mas, mas_sem.at[0])
    loads = [
        pltpu.make_async_copy(fst_in, fst, in_sem.at[0]),
        pltpu.make_async_copy(snd_in, snd, in_sem.at[1]),
    ]

    def saves(k):
        return [
            pltpu.make_async_copy(src.at[:, lanes(k)], dst.at[:, lanes(k)], out_sem.at[i, k])
            for i, (src, dst) in enumerate(((nm, nm_out), (nf, nf_out), (ns, ns_out)))
        ]

    load(0).start()
    def share(e, s):
        return jnp.where(holder[s] == e, 1.0, 0.0)

    barrier = pltpu.get_barrier_semaphore()
    peers = [(p, v) for v in to_z[1:] + to_y[1:]] + [(v, q) for v in to_x[1:]] + [(other, q)]
    for peer in peers:
        pl.semaphore_signal(barrier, inc=1, device_id=peer, device_id_type=MESH)
    for k in range(1, chunks):
        load(k).start()
    load_mas.start()
    for yy in range(ny):
        load_hid(yy).start()
    for copy in loads:
        copy.start()
    pl.semaphore_wait(barrier, len(peers))

    def meta_copy(j):
        return remote(meta.at[at_z[j]], mz.at[z], ms.at[0], mr.at[0], p, to_z[j])

    def meta_all():
        return remote(meta.at[pl.ds(0, nz - 1)], mz.at[pl.ds(0, nz - 1)], ms.at[0], mr.at[0], p, to_z[1])

    def rel_copy(j):
        return remote(rel.at[at_y[j]], relr.at[y], rs.at[0], rr.at[0], p, to_y[j])

    def rel_all():
        return remote(rel.at[pl.ds(0, ny - 1)], relr.at[pl.ds(0, ny - 1)], rs.at[0], rr.at[0], p, to_y[1])

    def ret_copy(j):
        return remote(ret.at[at_y[j]], retr.at[y], qs.at[0], qr.at[0], p, to_y[j])

    def ret_all():
        return remote(ret.at[pl.ds(0, ny - 1)], retr.at[pl.ds(0, ny - 1)], qs.at[0], qr.at[0], p, to_y[1])

    def back_copy(j):
        return remote(bz.at[at_z[j]], bk.at[z], bs.at[0], br.at[0], p, to_z[j])

    def back_all():
        return remote(bz.at[pl.ds(0, nz - 1)], bk.at[pl.ds(0, nz - 1)], bs.at[0], br.at[0], p, to_z[1])

    origins = ([at_z[-h % nz] for h in range(far)], [at_z[h % nz] for h in range(far)])
    nexts = (to_z[1], to_z[nz - 1])

    def hop(d, h, k):
        if isinstance(d, int):
            origin, to = origins[d][h - 1], nexts[d]
        else:
            origin = jnp.where(d == 0, origins[0][h - 1], origins[1][h - 1])
            to = jnp.where(d == 0, nexts[0], nexts[1])
        return remote(xg.at[k, origin], xg.at[k, origin], zs.at[d, h - 1, k], zr.at[d, h - 1, k], p, to)

    def forward(h, k, wait):
        for d in (0, 1):
            if h <= near:
                if wait:
                    hop(d, h, k).wait()
                if h + 1 <= near:
                    hop(d, h + 1, k).start()
        if h == near and near < far:
            hop(lax.rem(k, 2), far, k).start()
        if h > near and wait:
            hop(lax.rem(k, 2), far, k).wait()

    cut = max(1, chunks // 2)
    pieces = [(0, cut), (cut, chunks - cut)]

    def weight_copy(j, i):
        here = pl.ds(*pieces[i])
        return remote(wg.at[here, c, x], wg.at[here, c, x], wxs.at[i], wxr.at[i], to_x[j], q)

    def weight_all(i):
        here, most = pl.ds(*pieces[i]), pl.ds(0, nx - 1)
        return remote(wg.at[here, c, most], wg.at[here, c, most], wxs.at[i], wxr.at[i], to_x[1], q)

    def weight_pass(i):
        here = pl.ds(*pieces[i])
        return remote(wg.at[here, c], wg.at[here, c], wcs.at[i], wcr.at[i], other, q)

    def row_copy(j, k, slot):
        return remote(sendy.at[slot, at_y[j]], rows.at[k, y], ys.at[k], yr.at[k], p, to_y[j])

    def row_all(k):
        most = pl.ds(0, ny - 1)
        return remote(sendy.at[0, most], rows.at[k, most], ys.at[k], yr.at[k], p, to_y[1])

    def core_copy(k):
        return remote(csend.at[lax.rem(k, SLACK)], crecv.at[k], cs.at[k], cr.at[k], other, q)

    def x_copy(j, k):
        return remote(
            xsend.at[lax.rem(k, SLACK), at_x[j]], xrecv.at[k, x], xs.at[k], xr.at[k], to_x[j], q
        )

    def x_all(k):
        most = pl.ds(0, nx - 1)
        return remote(xsend.at[0, most], xrecv.at[k, most], xs.at[k], xr.at[k], to_x[1], q)

    def first_copy(j, k, n):
        here = pl.ds(k, n)
        return remote(hs1.at[here, at_z[j]], hr1.at[here, z], h1s.at[k], h1r.at[k], p, to_z[j])

    def first_all(k, n):
        here, most = pl.ds(k, n), pl.ds(0, nz - 1)
        return remote(hs1.at[here, most], hr1.at[here, most], h1s.at[k], h1r.at[k], p, to_z[1])

    def table_copy(j, k, n):
        here = pl.ds(k, n)
        return remote(ts.at[here], tr.at[here, y], tss.at[k], tsr.at[k], p, to_y[j])

    def table_all(k, n):
        here, most = pl.ds(k, n), pl.ds(0, ny - 1)
        return remote(tr.at[here, most], tr.at[here, most], tss.at[k], tsr.at[k], p, to_y[1])

    def second_copy(j, k, n):
        here = pl.ds(k, n)
        return remote(hs2.at[here, at_z[j]], hr2.at[here, z], h2s.at[k], h2r.at[k], p, to_z[j])

    def second_all(k, n):
        here, most = pl.ds(k, n), pl.ds(0, nz - 1)
        return remote(hs2.at[here, most], hr2.at[here, most], h2s.at[k], h2r.at[k], p, to_z[1])

    def when(k):
        return pl.when((k >= 0) & (k < chunks))

    def grouped(k):
        def run(body):
            pl.when((k >= 0) & (k < chunks) & (lax.rem(k, 2) == 1))(lambda: body(k - 1, 2))
            if chunks % 2:
                pl.when(k == chunks - 1)(lambda: body(chunks - 1, 1))

        return run

    spot_row = lax.broadcasted_iota(jnp.int32, (cap, toks), 0).astype(F32)

    def step_of(k):
        flag = share(0, q)
        for e in range(1, HOT):
            flag = flag + share(e, q)

        @pl.when(k == 0)
        def _():
            for copy in loads:
                copy.wait()

        def adam(b, carry):
            here = pl.ds(pl.multiple_of(b * part, part), part)
            grad = flag * hr2[k, b].astype(F32) + (1.0 - flag) * gsh[k, here, :]
            old = mas[here, lanes(k)]
            first = beta_one * fst[here, lanes(k)].astype(F32) + (1.0 - beta_one) * grad
            second = beta_two * snd[here, lanes(k)].astype(F32) + (1.0 - beta_two) * grad * grad
            update = first / correct_one / (jnp.sqrt(second / correct_two) + epsilon) + decay_rate * old
            nm[here, lanes(k)] = old - learn_rate * update
            nf[here, lanes(k)] = first.astype(BF)
            ns[here, lanes(k)] = second.astype(BF)
            return carry

        lax.fori_loop(0, nz, adam, 0)
        for copy in saves(k):
            copy.start()


    def step(tau, carry):
        for h in range(far, 0, -1):

            @when(tau - AHEAD - h)
            def _(h=h, k=tau - AHEAD - h):
                forward(h, k, True)

        @when(tau)
        def _(k=tau):
            load(k).wait()
            for d in (0, 1):
                if near:
                    hop(d, 1, k).start()
            if not near:
                hop(lax.rem(k, 2), 1, k).start()

        @pl.when(tau == AHEAD)
        def _():
            load_mas.wait()
            for k in range(chunks):
                wg[k, c, x] = mas[:, k * dk : (k + 1) * dk].astype(BF)
            for i in (0, 1):
                for j in range(1, nx):
                    weight_copy(j, i).start()

        for i, at in ((0, picked + SLACK - 2), (1, picked + SLACK - 1 + cut // 2)):

            @pl.when(tau == at)
            def _(i=i):
                if nx > 1:
                    weight_all(i).wait()
                weight_pass(i).start()

        @pl.when(tau == AHEAD)
        def _():
            slots = nz * ny
            named = route[...]

            def count(s, carry):
                return carry + jnp.where(named == holder[s], 1.0, 0.0)

            copies = lax.fori_loop(0, slots, count, jnp.zeros(named.shape, F32))
            wanted = pick[...].astype(F32)
            wanted = wanted - copies * jnp.floor((wanted + 0.5) / copies)
            gates = prob[...].astype(BF).astype(F32)
            meta[...] = jnp.zeros_like(meta)

            def assign(s, seen):
                host = jnp.where(named == holder[s], 1.0, 0.0)
                hit = host * jnp.where(seen == wanted, 1.0, 0.0)
                chosen[s] = hit
                taken[pl.ds(s, 1), :] = jnp.sum(hit, axis=0, keepdims=True)
                meta[s // ny, pl.ds(ny + lax.rem(s, ny), 1), :] = jnp.sum(hit * gates, axis=0, keepdims=True)
                return seen + host

            lax.fori_loop(0, slots, assign, jnp.zeros(named.shape, F32))
            before = jnp.where(
                lax.broadcasted_iota(jnp.int32, (toks, toks), 0)
                < lax.broadcasted_iota(jnp.int32, (toks, toks), 1),
                1.0,
                0.0,
            ).astype(BF)
            place = jnp.dot(taken[...].astype(BF), before, preferred_element_type=F32)
            spot = jnp.where(taken[...] > 0.5, place, -1.0)
            for s in range(slots):
                meta[s // ny, s % ny : s % ny + 1, :] = spot[s : s + 1, :]
            for j in range(1, nz):
                meta_copy(j).start()
            mz[z] = meta[z]

        @pl.when(tau == AHEAD + 1)
        def _():
            meta_all().wait()
            for yy in range(ny):
                for zz in range(nz):
                    rel[yy, zz : zz + 1, :] = mz[zz, yy : yy + 1, :]
                    rel[yy, nz + zz : nz + zz + 1, :] = mz[zz, ny + yy : ny + yy + 1, :]
            for j in range(1, ny):
                rel_copy(j).start()
            relr[y] = rel[y]
            zero = jnp.zeros((cap, toks), F32)
            for jj in range(nz // 2):
                for yy in range(ny):
                    one = [
                        jnp.where(mz[2 * jj + i, yy : yy + 1, :] == spot_row, 1.0, 0.0) for i in (0, 1)
                    ]
                    top = jnp.concatenate([one[0], zero], axis=1)
                    low = jnp.concatenate([zero, one[1]], axis=1)
                    pick2[jj, yy * pair : (yy + 1) * pair, :] = jnp.concatenate([top, low], axis=0).astype(BF)

        begin, room = AHEAD + 2, picked + SLACK - AHEAD - 2

        @pl.when(tau == begin)
        def _():
            rel_all().wait()
            for yy in range(ny):
                load_hid(yy).wait()

        for yy in range(ny):

            @pl.when(tau == begin + yy * (room - 1) // ny)
            def _(yy=yy):
                def scale(zz, carry):
                    here = pl.ds(pl.multiple_of(yy * block + zz * cap, 8), cap)
                    hit = relr[yy, pl.ds(zz, 1), :] == spot_row
                    gate = jnp.where(hit, relr[yy, pl.ds(nz + zz, 1), :], 0.0)
                    column = jnp.sum(gate, axis=1, keepdims=True)
                    gcol[here, :] = jnp.broadcast_to(column, (cap, 128))
                    proj[here, :] = hid[yy, zz].astype(F32) * column
                    return carry

                lax.fori_loop(0, nz, scale, 0)

        @pl.when(tau == begin + room - 1)
        def _():
            def turn(i, carry):
                here = pl.ds(pl.multiple_of(i * 128, 128), 128)
                turned = proj[here, :].T.astype(BF)
                for core in range(CORES):
                    for xx in range(nx):
                        start = (xx * CORES + core) * shard
                        gated[core, xx * shard : (xx + 1) * shard, here] = turned[start : start + shard, :]
                return carry

            lax.fori_loop(0, ny * block // 128, turn, 0)
            proj[...] = jnp.zeros_like(proj)

        @when(tau - picked)
        def _(k=tau - picked):
            slot = lax.rem(k, SLACK + 1)

            def choose(jj, carry):
                two = xg[k, pl.ds(2 * jj, 2)].reshape(2 * toks, dk)
                got = jnp.dot(pick2[jj], two, preferred_element_type=F32).astype(BF)
                here = pl.ds(pl.multiple_of(jj * pair, pair), pair)
                for yy in range(ny):
                    sendy[slot, yy, here, :] = got[yy * pair : (yy + 1) * pair, :]
                return carry

            lax.fori_loop(0, nz // 2, choose, 0)
            for j in range(1, ny):
                row_copy(j, k, slot).start()
            rows[k, y] = sendy[slot, y]

        @grouped(tau - picked - 5 * SLACK)
        def _(k0, n):
            table_all(k0, n).wait()
            for i in range(n):
                k = k0 + i
                total = []
                for e in range(HOT):
                    acc = tr[k, 0, e].astype(F32)
                    for yy in range(1, ny):
                        acc = acc + tr[k, yy, e].astype(F32)
                    total.append(acc)
                for zz in range(nz):
                    acc = share(0, zz * ny + y) * total[0]
                    for e in range(1, HOT):
                        acc = acc + share(e, zz * ny + y) * total[e]
                    hs2[k, zz] = acc.astype(BF)
            for j in range(1, nz):
                second_copy(j, k0, n).start()
            for i in range(n):
                hr2[k0 + i, z] = hs2[k0 + i, z]

        @grouped(tau - picked - 4 * SLACK)
        def _(k0, n):
            first_all(k0, n).wait()
            for i in range(n):
                k = k0 + i
                sums = [jnp.zeros((part, dk), F32)] * HOT
                for zz in range(nz):
                    value = hr1[k, zz].astype(F32)
                    sums = [sums[e] + share(e, zz * ny + y) * value for e in range(HOT)]
                for e in range(HOT):
                    ts[k, e] = sums[e].astype(BF)
            for j in range(1, ny):
                table_copy(j, k0, n).start()
            for i in range(n):
                tr[k0 + i, y] = ts[k0 + i]

        @when(tau - picked - 3 * SLACK)
        def _(k=tau - picked - 3 * SLACK):
            if nx > 1:
                x_all(k).wait()

            def add(b, carry):
                here = pl.ds(pl.multiple_of(b * part, part), part)
                value = xown[lax.rem(k, SLACK), here, :]
                for j in range(1, nx):
                    value = value + xrecv[k, at_x[nx - j], here, :].astype(F32)
                gsh[k, here, :] = value
                hs1[k, b] = value.astype(BF)
                return carry

            lax.fori_loop(0, nz, add, 0)
            hr1[k, z] = hs1[k, z]

        @grouped(tau - picked - 3 * SLACK)
        def _(k0, n):
            for j in range(1, nz):
                first_copy(j, k0, n).start()

        @when(tau - picked - 2 * SLACK)
        def _(k=tau - picked - 2 * SLACK):
            slot = lax.rem(k, SLACK)
            core_copy(k).wait()
            for j in range(1, nx):
                xsend[slot, at_x[j]] = (
                    ownh[slot, at_x[j]].astype(F32) + crecv[k, at_x[j]].astype(F32)
                ).astype(BF)
                x_copy(j, k).start()
            xown[slot] = ownh[slot, x].astype(F32) + crecv[k, x].astype(F32)

        @when(tau - picked - 1 * SLACK)
        def _(k=tau - picked - 1 * SLACK):
            row_all(k).wait()
            slot = lax.rem(k, SLACK)

            tile = min(256, dk)

            def half(core, out):
                def columns(t, carry):
                    here = pl.ds(pl.multiple_of(t * tile, tile), tile)
                    got = jnp.dot(
                        gated[core],
                        rows[k, :, :, here].reshape(ny * block, tile),
                        preferred_element_type=F32,
                    )
                    out[slot, :, :, here] = got.astype(BF).reshape(nx, shard, tile)
                    return carry

                lax.fori_loop(0, dk // tile, columns, 0)

            def project(xx, carry):
                w = jnp.concatenate([wg[k, 0, xx], wg[k, 1, xx]], axis=0)
                here = pl.ds(pl.multiple_of(xx * CORES * shard, CORES * shard), CORES * shard)
                proj[:, here] += lax.dot_general(
                    rows[k].reshape(ny * block, dk), w, (((1,), (1,)), ((), ())), preferred_element_type=F32
                )
                return carry

            half(1 - c, csend)
            core_copy(k).start()
            half(c, ownh)
            for i in (0, 1):

                @pl.when(k == pieces[i][0])
                def _(i=i):
                    weight_pass(i).wait()

            lax.fori_loop(0, nx, project, 0)

        @grouped(tau - picked - 6 * SLACK)
        def _(k0, n):
            second_all(k0, n).wait()
            for i in range(n):
                step_of(k0 + i)

        last = chunks + picked + SLACK

        for yy in range(ny):

            @pl.when(tau == last + yy)
            def _(yy=yy):
                def finish(zz, carry):
                    here = pl.ds(pl.multiple_of(yy * block + zz * cap, 8), cap)
                    value = proj[here, :]
                    hg[yy, zz] = (gcol[here, :][:, 0:1] * value).astype(BF)
                    term = jnp.sum(hid[yy, zz].astype(F32) * value, axis=1, keepdims=True)
                    hit = relr[yy, pl.ds(zz, 1), :] == spot_row
                    ret[yy, pl.ds(zz, 1), :] = jnp.sum(jnp.where(hit, term, 0.0), axis=0, keepdims=True)
                    return carry

                lax.fori_loop(0, nz, finish, 0)
                save_hg(yy).start()

        @pl.when(tau == last + ny - 1)
        def _():
            for j in range(1, ny):
                ret_copy(j).start()
            retr[y] = ret[y]

        @pl.when(tau == last + ny)
        def _():
            ret_all().wait()
            bz[...] = jnp.zeros_like(bz)
            for zz in range(nz):
                for yy in range(ny):
                    bz[zz, yy : yy + 1, :] = retr[yy, zz : zz + 1, :]
            for j in range(1, nz):
                back_copy(j).start()
            bk[z] = bz[z]

        @pl.when(tau == last + ny + 1)
        def _():
            back_all().wait()
            total = jnp.zeros(gg.shape, F32)
            for s in range(nz * ny):
                total = total + chosen[s] * bk[s // ny, s % ny : s % ny + 1, :]
            gg[...] = total

        return carry

    lax.fori_loop(0, chunks + picked + max(6 * SLACK, SLACK + ny + 2), step, 0)
    for k in range(chunks):
        for copy in saves(k):
            copy.wait()
    for yy in range(ny):
        save_hg(yy).wait()


def whole(nx, ny, nz, chunks, holder, route, pick, prob, tok, hid, mas, fst, snd):
    toks, feats = tok.shape
    dk = feats // chunks
    shard = mas.shape[0]
    cap, units = hid.shape[2:]
    slots = nz * ny
    count = slots * cap
    block = nz * cap
    part = shard // nz
    top = route.shape[0]
    hbm = pl.BlockSpec(memory_space=pl.ANY)
    vmem = pl.BlockSpec(memory_space=pltpu.VMEM)
    dma = pltpu.SemaphoreType.DMA
    n_dma = lambda *s: dma(tuple(max(1, v) for v in s))
    scratch = [
        pltpu.VMEM((ny, nz, cap, units), BF),
        pltpu.VMEM((shard, feats), F32),
        pltpu.VMEM((shard, feats), BF),
        pltpu.VMEM((shard, feats), BF),
        pltpu.VMEM((ny, nz, cap, units), BF),
        pltpu.VMEM((shard, feats), F32),
        pltpu.VMEM((shard, feats), BF),
        pltpu.VMEM((shard, feats), BF),
        pltpu.VMEM((slots, top, toks), F32),
        pltpu.VMEM((slots, toks), F32),
        pltpu.VMEM((nz, 8, toks), F32),
        pltpu.VMEM((chunks, nz, toks, dk), BF),
        pltpu.VMEM((chunks, CORES, nx, shard, dk), BF),
        pltpu.VMEM((SLACK + 1, ny, block, dk), BF),
        pltpu.VMEM((chunks, ny, block, dk), BF),
        pltpu.VMEM((nz // 2, ny * 2 * cap, 2 * toks), BF),
        pltpu.VMEM((count, 128), F32),
        pltpu.VMEM((CORES, units // CORES, count), BF),
        pltpu.VMEM((count, units), F32),
        pltpu.VMEM((SLACK, nx, shard, dk), BF),
        pltpu.VMEM((chunks, nx, shard, dk), BF),
        pltpu.VMEM((SLACK, nx, shard, dk), BF),
        pltpu.VMEM((SLACK, nx, shard, dk), BF),
        pltpu.VMEM((chunks, nx, shard, dk), BF),
        pltpu.VMEM((SLACK, shard, dk), F32),
        pltpu.VMEM((chunks, shard, dk), F32),
        pltpu.VMEM((chunks, nz, part, dk), BF),
        pltpu.VMEM((chunks, nz, part, dk), BF),
        pltpu.VMEM((chunks, HOT, part, dk), BF),
        pltpu.VMEM((chunks, ny, HOT, part, dk), BF),
        pltpu.VMEM((chunks, nz, part, dk), BF),
        pltpu.VMEM((chunks, nz, part, dk), BF),
        pltpu.VMEM((nz, 8, 128), F32),
        pltpu.VMEM((ny, 2 * nz, 128), F32),
        pltpu.VMEM((ny, 2 * nz, 128), F32),
        pltpu.VMEM((ny, nz, 128), F32),
        pltpu.VMEM((ny, nz, 128), F32),
        pltpu.VMEM((nz, 8, 128), F32),
        pltpu.VMEM((nz, 8, 128), F32),
        n_dma(chunks),
        n_dma(chunks),
        n_dma(2),
        n_dma(ny),
        n_dma(3, chunks),
        n_dma(ny),
        n_dma(2, nz // 2, chunks),
        n_dma(2, nz // 2, chunks),
        n_dma(chunks),
        n_dma(chunks),
        n_dma(chunks),
        n_dma(chunks),
        n_dma(chunks),
        n_dma(chunks),
        n_dma(chunks),
        n_dma(chunks),
        n_dma(chunks),
        n_dma(chunks),
        n_dma(chunks),
        n_dma(chunks),
        n_dma(chunks),
        n_dma(chunks),
        n_dma(chunks),
        n_dma(chunks),
        n_dma(1),
        n_dma(1),
        n_dma(1),
        n_dma(1),
        n_dma(1),
        n_dma(1),
        n_dma(1),
        n_dma(1),
    ]
    return pl.pallas_call(
        functools.partial(kernel, nx, ny, nz, chunks, cap),
        out_shape=(
            jax.ShapeDtypeStruct((nz, ny, cap, units), BF),
            jax.ShapeDtypeStruct((top, toks), F32),
            jax.ShapeDtypeStruct((shard, feats), F32),
            jax.ShapeDtypeStruct((shard, feats), BF),
            jax.ShapeDtypeStruct((shard, feats), BF),
        ),
        in_specs=[pl.BlockSpec(memory_space=pltpu.SMEM), vmem, vmem, vmem, hbm, hbm, hbm, hbm, hbm],
        out_specs=(hbm, vmem, hbm, hbm, hbm),
        scratch_shapes=scratch,
        compiler_params=pltpu.CompilerParams(
            collective_id=0, has_side_effects=True, vmem_limit_bytes=62 * 2**20
        ),
        cost_estimate=pl.CostEstimate(
            flops=4 * count * units * feats, bytes_accessed=20 * 2**20, transcendentals=0
        ),
    )(holder, route, pick, prob, tok, hid, mas, fst, snd)


def on_device(
    nx,
    ny,
    nz,
    chunks,
    grad_out,
    gate_probs,
    expert_route,
    replica_pick,
    slot_expert,
    saved_hidden,
    master,
    first_moment,
    second_moment,
):
    cap, units = saved_hidden.shape[4:]
    hidden_grad, gate_grad, new_master, new_first, new_second = whole(
        nx,
        ny,
        nz,
        chunks,
        slot_expert,
        expert_route.T,
        replica_pick.T,
        gate_probs.T,
        grad_out,
        saved_hidden.reshape(nz, ny, cap, units),
        master[0],
        first_moment[0],
        second_moment[0],
    )
    return (
        hidden_grad.reshape(saved_hidden.shape),
        gate_grad.T,
        new_master[None],
        new_first[None],
        new_second[None],
    )


def build(mesh, nx, ny, nz, chunks):
    tokens = P(("dp", "expert"), None)
    acts = P("dp", "expert", None, None, None, None)
    shard = P("expert", "dp", None)
    return jax.shard_map(
        functools.partial(on_device, nx, ny, nz, chunks),
        mesh=mesh,
        in_specs=(tokens, tokens, tokens, tokens, P(), acts, shard, shard, shard),
        out_specs=(acts, tokens, shard, shard, shard),
        check_vma=False,
    )


def solution(mesh):
    ny = 4
    return build(mesh, mesh.shape["dp"] // CORES, ny, mesh.shape["expert"] // ny, 7)
```

```python
import functools

import jax
import jax.numpy as jnp
from jax import lax
from jax.experimental import pallas as pl
from jax.experimental.pallas import tpu as pltpu
from jax.sharding import PartitionSpec as P

HOT = 3
CORES = 2
AHEAD = 1
SLACK = 2
BF = jnp.bfloat16
F32 = jnp.float32
MESH = pl.DeviceIdType.MESH

beta_one = 0.9
beta_two = 0.95
learn_rate = 0.00022
decay_rate = 0.1
epsilon = 1e-08
correct_one = 0.6513215599
correct_two = 0.4012630607


def kernel(
    nx,
    ny,
    nz,
    chunks,
    cap,
    holder,
    route,
    pick,
    prob,
    tok,
    hid_in,
    mas_in,
    fst_in,
    snd_in,
    hg_out,
    gg,
    nm_out,
    nf_out,
    ns_out,
    hid,
    mas,
    fst,
    snd,
    hg,
    nm,
    nf,
    ns,
    chosen,
    taken,
    meta,
    xg,
    wg,
    sendy,
    rows,
    pick2,
    gcol,
    gated,
    proj,
    csend,
    crecv,
    ownh,
    xsend,
    xrecv,
    xown,
    gsh,
    hs1,
    hr1,
    ts,
    tr,
    hs2,
    hr2,
    mz,
    rel,
    relr,
    ret,
    retr,
    bz,
    bk,
    load_sem,
    mas_sem,
    in_sem,
    hid_sem,
    out_sem,
    hg_sem,
    zs,
    zr,
    ys,
    yr,
    wxs,
    wxr,
    wcs,
    wcr,
    cs,
    cr,
    xs,
    xr,
    h1s,
    h1r,
    tss,
    tsr,
    h2s,
    h2r,
    ms,
    mr,
    rs,
    rr,
    qs,
    qr,
    bs,
    br,
):
    p, q = lax.axis_index("dp"), lax.axis_index("expert")
    x, c = p // CORES, lax.rem(p, CORES)
    z, y = q // ny, lax.rem(q, ny)
    toks = xg.shape[2]
    dk = xg.shape[3]
    shard = wg.shape[3]
    far, near = nz // 2, nz - 1 - nz // 2
    block = nz * cap
    pair = 2 * cap
    part = shard // nz
    picked = far + AHEAD

    at_x = [lax.rem(x + j, nx) for j in range(nx)]
    at_y = [lax.rem(y + j, ny) for j in range(ny)]
    at_z = [lax.rem(z + j, nz) for j in range(nz)]
    to_x = [v * CORES + c for v in at_x]
    to_y = [z * ny + v for v in at_y]
    to_z = [v * ny + y for v in at_z]
    other = x * CORES + 1 - c

    def remote(src, dst, ssem, rsem, pp, qq):
        return pltpu.make_async_remote_copy(
            src_ref=src, dst_ref=dst, send_sem=ssem, recv_sem=rsem, device_id=(pp, qq), device_id_type=MESH
        )

    def lanes(k):
        return pl.ds(pl.multiple_of(k * dk, 128), dk)

    def load(k):
        return pltpu.make_async_copy(tok.at[:, lanes(k)], xg.at[k, z], load_sem.at[k])

    def load_hid(yy):
        return pltpu.make_async_copy(hid_in.at[:, yy], hid.at[yy], hid_sem.at[yy])

    def save_hg(yy):
        return pltpu.make_async_copy(hg.at[yy], hg_out.at[:, yy], hg_sem.at[yy])

    load_mas = pltpu.make_async_copy(mas_in, mas, mas_sem.at[0])
    loads = [
        pltpu.make_async_copy(fst_in, fst, in_sem.at[0]),
        pltpu.make_async_copy(snd_in, snd, in_sem.at[1]),
    ]

    def saves(k):
        return [
            pltpu.make_async_copy(src.at[:, lanes(k)], dst.at[:, lanes(k)], out_sem.at[i, k])
            for i, (src, dst) in enumerate(((nm, nm_out), (nf, nf_out), (ns, ns_out)))
        ]

    load(0).start()
    def share(e, s):
        return jnp.where(holder[s] == e, 1.0, 0.0)

    barrier = pltpu.get_barrier_semaphore()
    peers = [(p, v) for v in to_z[1:] + to_y[1:]] + [(v, q) for v in to_x[1:]] + [(other, q)]
    for peer in peers:
        pl.semaphore_signal(barrier, inc=1, device_id=peer, device_id_type=MESH)
    for k in range(1, chunks):
        load(k).start()
    load_mas.start()
    for yy in range(ny):
        load_hid(yy).start()
    for copy in loads:
        copy.start()
    pl.semaphore_wait(barrier, len(peers))

    def meta_copy(j):
        return remote(meta.at[at_z[j]], mz.at[z], ms.at[0], mr.at[0], p, to_z[j])

    def meta_all():
        return remote(meta.at[pl.ds(0, nz - 1)], mz.at[pl.ds(0, nz - 1)], ms.at[0], mr.at[0], p, to_z[1])

    def rel_copy(j):
        return remote(rel.at[at_y[j]], relr.at[y], rs.at[0], rr.at[0], p, to_y[j])

    def rel_all():
        return remote(rel.at[pl.ds(0, ny - 1)], relr.at[pl.ds(0, ny - 1)], rs.at[0], rr.at[0], p, to_y[1])

    def ret_copy(j):
        return remote(ret.at[at_y[j]], retr.at[y], qs.at[0], qr.at[0], p, to_y[j])

    def ret_all():
        return remote(ret.at[pl.ds(0, ny - 1)], retr.at[pl.ds(0, ny - 1)], qs.at[0], qr.at[0], p, to_y[1])

    def back_copy(j):
        return remote(bz.at[at_z[j]], bk.at[z], bs.at[0], br.at[0], p, to_z[j])

    def back_all():
        return remote(bz.at[pl.ds(0, nz - 1)], bk.at[pl.ds(0, nz - 1)], bs.at[0], br.at[0], p, to_z[1])

    origins = ([at_z[-h % nz] for h in range(far)], [at_z[h % nz] for h in range(far)])
    nexts = (to_z[1], to_z[nz - 1])

    def hop(d, h, k):
        if isinstance(d, int):
            origin, to = origins[d][h - 1], nexts[d]
        else:
            origin = jnp.where(d == 0, origins[0][h - 1], origins[1][h - 1])
            to = jnp.where(d == 0, nexts[0], nexts[1])
        return remote(xg.at[k, origin], xg.at[k, origin], zs.at[d, h - 1, k], zr.at[d, h - 1, k], p, to)

    def forward(h, k, wait):
        for d in (0, 1):
            if h <= near:
                if wait:
                    hop(d, h, k).wait()
                if h + 1 <= near:
                    hop(d, h + 1, k).start()
        if h == near and near < far:
            hop(lax.rem(k, 2), far, k).start()
        if h > near and wait:
            hop(lax.rem(k, 2), far, k).wait()

    cut = max(1, chunks // 2)
    pieces = [(0, cut), (cut, chunks - cut)]

    def weight_copy(j, i):
        here = pl.ds(*pieces[i])
        return remote(wg.at[here, c, x], wg.at[here, c, x], wxs.at[i], wxr.at[i], to_x[j], q)

    def weight_all(i):
        here, most = pl.ds(*pieces[i]), pl.ds(0, nx - 1)
        return remote(wg.at[here, c, most], wg.at[here, c, most], wxs.at[i], wxr.at[i], to_x[1], q)

    def weight_pass(i):
        here = pl.ds(*pieces[i])
        return remote(wg.at[here, c], wg.at[here, c], wcs.at[i], wcr.at[i], other, q)

    def row_copy(j, k, slot, here):
        return remote(sendy.at[slot, at_y[j], here], rows.at[k, y, here], ys.at[k], yr.at[k], p, to_y[j])

    def row_all(k):
        most = pl.ds(0, ny - 1)
        return remote(sendy.at[0, most], rows.at[k, most], ys.at[k], yr.at[k], p, to_y[1])

    def core_copy(k):
        return remote(csend.at[lax.rem(k, SLACK)], crecv.at[k], cs.at[k], cr.at[k], other, q)

    def x_copy(j, k):
        return remote(
            xsend.at[lax.rem(k, SLACK), at_x[j]], xrecv.at[k, x], xs.at[k], xr.at[k], to_x[j], q
        )

    def x_all(k):
        most = pl.ds(0, nx - 1)
        return remote(xsend.at[0, most], xrecv.at[k, most], xs.at[k], xr.at[k], to_x[1], q)

    def first_copy(j, k, n):
        here = pl.ds(k, n)
        return remote(hs1.at[here, at_z[j]], hr1.at[here, z], h1s.at[k], h1r.at[k], p, to_z[j])

    def first_all(k, n):
        here, most = pl.ds(k, n), pl.ds(0, nz - 1)
        return remote(hs1.at[here, most], hr1.at[here, most], h1s.at[k], h1r.at[k], p, to_z[1])

    def table_copy(j, k, n):
        here = pl.ds(k, n)
        return remote(ts.at[here], tr.at[here, y], tss.at[k], tsr.at[k], p, to_y[j])

    def table_all(k, n):
        here, most = pl.ds(k, n), pl.ds(0, ny - 1)
        return remote(tr.at[here, most], tr.at[here, most], tss.at[k], tsr.at[k], p, to_y[1])

    def second_copy(j, k, n):
        here = pl.ds(k, n)
        return remote(hs2.at[here, at_z[j]], hr2.at[here, z], h2s.at[k], h2r.at[k], p, to_z[j])

    def second_all(k, n):
        here, most = pl.ds(k, n), pl.ds(0, nz - 1)
        return remote(hs2.at[here, most], hr2.at[here, most], h2s.at[k], h2r.at[k], p, to_z[1])

    def when(k):
        return pl.when((k >= 0) & (k < chunks))

    def grouped(k):
        def run(body):
            pl.when((k >= 0) & (k < chunks) & (lax.rem(k, 2) == 1))(lambda: body(k - 1, 2))
            if chunks % 2:
                pl.when(k == chunks - 1)(lambda: body(chunks - 1, 1))

        return run

    spot_row = lax.broadcasted_iota(jnp.int32, (cap, toks), 0).astype(F32)

    def step_of(k):
        flag = share(0, q)
        for e in range(1, HOT):
            flag = flag + share(e, q)

        @pl.when(k == 0)
        def _():
            for copy in loads:
                copy.wait()

        def adam(b, carry):
            here = pl.ds(pl.multiple_of(b * part, part), part)
            grad = flag * hr2[k, b].astype(F32) + (1.0 - flag) * gsh[k, here, :]
            old = mas[here, lanes(k)]
            first = beta_one * fst[here, lanes(k)].astype(F32) + (1.0 - beta_one) * grad
            second = beta_two * snd[here, lanes(k)].astype(F32) + (1.0 - beta_two) * grad * grad
            update = first / correct_one / (jnp.sqrt(second / correct_two) + epsilon) + decay_rate * old
            nm[here, lanes(k)] = old - learn_rate * update
            nf[here, lanes(k)] = first.astype(BF)
            ns[here, lanes(k)] = second.astype(BF)
            return carry

        lax.fori_loop(0, nz, adam, 0)
        for copy in saves(k):
            copy.start()


    def step(tau, carry):
        for h in range(far, 0, -1):

            @when(tau - AHEAD - h)
            def _(h=h, k=tau - AHEAD - h):
                forward(h, k, True)

        @when(tau)
        def _(k=tau):
            load(k).wait()
            for d in (0, 1):
                if near:
                    hop(d, 1, k).start()
            if not near:
                hop(lax.rem(k, 2), 1, k).start()

        @pl.when(tau == AHEAD)
        def _():
            load_mas.wait()
            for k in range(chunks):
                wg[k, c, x] = mas[:, k * dk : (k + 1) * dk].astype(BF)
            for i in (0, 1):
                for j in range(1, nx):
                    weight_copy(j, i).start()

        for i, at in ((0, picked + SLACK - 2), (1, picked + SLACK - 1 + cut // 2)):

            @pl.when(tau == at)
            def _(i=i):
                if nx > 1:
                    weight_all(i).wait()
                weight_pass(i).start()

        @pl.when(tau == AHEAD)
        def _():
            slots = nz * ny
            named = route[...]

            def count(s, carry):
                return carry + jnp.where(named == holder[s], 1.0, 0.0)

            copies = lax.fori_loop(0, slots, count, jnp.zeros(named.shape, F32))
            wanted = pick[...].astype(F32)
            wanted = wanted - copies * jnp.floor((wanted + 0.5) / copies)
            gates = prob[...].astype(BF).astype(F32)
            meta[...] = jnp.zeros_like(meta)

            def assign(s, seen):
                host = jnp.where(named == holder[s], 1.0, 0.0)
                hit = host * jnp.where(seen == wanted, 1.0, 0.0)
                chosen[s] = hit
                taken[pl.ds(s, 1), :] = jnp.sum(hit, axis=0, keepdims=True)
                meta[s // ny, pl.ds(ny + lax.rem(s, ny), 1), :] = jnp.sum(hit * gates, axis=0, keepdims=True)
                return seen + host

            lax.fori_loop(0, slots, assign, jnp.zeros(named.shape, F32))
            before = jnp.where(
                lax.broadcasted_iota(jnp.int32, (toks, toks), 0)
                < lax.broadcasted_iota(jnp.int32, (toks, toks), 1),
                1.0,
                0.0,
            ).astype(BF)
            place = jnp.dot(taken[...].astype(BF), before, preferred_element_type=F32)
            spot = jnp.where(taken[...] > 0.5, place, -1.0)
            for s in range(slots):
                meta[s // ny, s % ny : s % ny + 1, :] = spot[s : s + 1, :]
            for j in range(1, nz):
                meta_copy(j).start()
            mz[z] = meta[z]

        @pl.when(tau == AHEAD + 1)
        def _():
            meta_all().wait()
            for yy in range(ny):
                for zz in range(nz):
                    rel[yy, zz : zz + 1, :] = mz[zz, yy : yy + 1, :]
                    rel[yy, nz + zz : nz + zz + 1, :] = mz[zz, ny + yy : ny + yy + 1, :]
            for j in range(1, ny):
                rel_copy(j).start()
            relr[y] = rel[y]
            zero = jnp.zeros((cap, toks), F32)
            for jj in range(nz // 2):
                for yy in range(ny):
                    one = [
                        jnp.where(mz[2 * jj + i, yy : yy + 1, :] == spot_row, 1.0, 0.0) for i in (0, 1)
                    ]
                    top = jnp.concatenate([one[0], zero], axis=1)
                    low = jnp.concatenate([zero, one[1]], axis=1)
                    pick2[jj, yy * pair : (yy + 1) * pair, :] = jnp.concatenate([top, low], axis=0).astype(BF)

        begin, room = AHEAD + 2, picked + SLACK - AHEAD - 2

        @pl.when(tau == begin)
        def _():
            rel_all().wait()
            for yy in range(ny):
                load_hid(yy).wait()

        for yy in range(ny):

            @pl.when(tau == begin + yy * (room - 1) // ny)
            def _(yy=yy):
                def scale(zz, carry):
                    here = pl.ds(pl.multiple_of(yy * block + zz * cap, 8), cap)
                    hit = relr[yy, pl.ds(zz, 1), :] == spot_row
                    gate = jnp.where(hit, relr[yy, pl.ds(nz + zz, 1), :], 0.0)
                    column = jnp.sum(gate, axis=1, keepdims=True)
                    gcol[here, :] = jnp.broadcast_to(column, (cap, 128))
                    proj[here, :] = hid[yy, zz].astype(F32) * column
                    return carry

                lax.fori_loop(0, nz, scale, 0)

        @pl.when(tau == begin + room - 1)
        def _():
            def turn(i, carry):
                here = pl.ds(pl.multiple_of(i * 128, 128), 128)
                turned = proj[here, :].T.astype(BF)
                for core in range(CORES):
                    for xx in range(nx):
                        start = (xx * CORES + core) * shard
                        gated[core, xx * shard : (xx + 1) * shard, here] = turned[start : start + shard, :]
                return carry

            lax.fori_loop(0, ny * block // 128, turn, 0)
            proj[...] = jnp.zeros_like(proj)

        def arrived(i, carry):
            h = far - i
            side = 2 * lax.rem(z, 2) - 1
            off = jnp.where(h == 1, 0, jnp.where(h == 2, side, jnp.where(h == 3, -side, 2)))
            jj = lax.rem(z // 2 + off + nz // 2, nz // 2)

            @when(tau - AHEAD - h)
            def _(k=tau - AHEAD - h):
                slot = lax.rem(k, far + SLACK)
                two = xg[k, pl.ds(2 * jj, 2)].reshape(2 * toks, dk)
                got = jnp.dot(pick2[jj], two, preferred_element_type=F32).astype(BF)
                here = pl.ds(pl.multiple_of(jj * pair, pair), pair)
                for yy in range(ny):
                    sendy[slot, yy, here, :] = got[yy * pair : (yy + 1) * pair, :]
                for j in range(1, ny):
                    row_copy(j, k, slot, here).start()
                rows[k, y, here, :] = sendy[slot, y, here, :]

            return carry

        lax.fori_loop(0, far, arrived, 0)

        @grouped(tau - picked - 5 * SLACK)
        def _(k0, n):
            table_all(k0, n).wait()
            for i in range(n):
                k = k0 + i
                total = []
                for e in range(HOT):
                    acc = tr[k, 0, e].astype(F32)
                    for yy in range(1, ny):
                        acc = acc + tr[k, yy, e].astype(F32)
                    total.append(acc)
                for zz in range(nz):
                    acc = share(0, zz * ny + y) * total[0]
                    for e in range(1, HOT):
                        acc = acc + share(e, zz * ny + y) * total[e]
                    hs2[k, zz] = acc.astype(BF)
            for j in range(1, nz):
                second_copy(j, k0, n).start()
            for i in range(n):
                hr2[k0 + i, z] = hs2[k0 + i, z]

        @grouped(tau - picked - 4 * SLACK)
        def _(k0, n):
            first_all(k0, n).wait()
            for i in range(n):
                k = k0 + i
                sums = [jnp.zeros((part, dk), F32)] * HOT
                for zz in range(nz):
                    value = hr1[k, zz].astype(F32)
                    sums = [sums[e] + share(e, zz * ny + y) * value for e in range(HOT)]
                for e in range(HOT):
                    ts[k, e] = sums[e].astype(BF)
            for j in range(1, ny):
                table_copy(j, k0, n).start()
            for i in range(n):
                tr[k0 + i, y] = ts[k0 + i]

        @when(tau - picked - 3 * SLACK)
        def _(k=tau - picked - 3 * SLACK):
            if nx > 1:
                x_all(k).wait()

            def add(b, carry):
                here = pl.ds(pl.multiple_of(b * part, part), part)
                value = xown[lax.rem(k, SLACK), here, :]
                for j in range(1, nx):
                    value = value + xrecv[k, at_x[nx - j], here, :].astype(F32)
                gsh[k, here, :] = value
                hs1[k, b] = value.astype(BF)
                return carry

            lax.fori_loop(0, nz, add, 0)
            hr1[k, z] = hs1[k, z]

        @grouped(tau - picked - 3 * SLACK)
        def _(k0, n):
            for j in range(1, nz):
                first_copy(j, k0, n).start()

        @when(tau - picked - 2 * SLACK)
        def _(k=tau - picked - 2 * SLACK):
            slot = lax.rem(k, SLACK)
            core_copy(k).wait()
            for j in range(1, nx):
                xsend[slot, at_x[j]] = (
                    ownh[slot, at_x[j]].astype(F32) + crecv[k, at_x[j]].astype(F32)
                ).astype(BF)
                x_copy(j, k).start()
            xown[slot] = ownh[slot, x].astype(F32) + crecv[k, x].astype(F32)

        @when(tau - picked - 1 * SLACK)
        def _(k=tau - picked - 1 * SLACK):
            row_all(k).wait()
            slot = lax.rem(k, SLACK)

            tile = min(256, dk)

            def half(core, out):
                def columns(t, carry):
                    here = pl.ds(pl.multiple_of(t * tile, tile), tile)
                    got = jnp.dot(
                        gated[core],
                        rows[k, :, :, here].reshape(ny * block, tile),
                        preferred_element_type=F32,
                    )
                    out[slot, :, :, here] = got.astype(BF).reshape(nx, shard, tile)
                    return carry

                lax.fori_loop(0, dk // tile, columns, 0)

            def project(xx, carry):
                w = jnp.concatenate([wg[k, 0, xx], wg[k, 1, xx]], axis=0)
                here = pl.ds(pl.multiple_of(xx * CORES * shard, CORES * shard), CORES * shard)
                proj[:, here] += lax.dot_general(
                    rows[k].reshape(ny * block, dk), w, (((1,), (1,)), ((), ())), preferred_element_type=F32
                )
                return carry

            half(1 - c, csend)
            core_copy(k).start()
            half(c, ownh)
            for i in (0, 1):

                @pl.when(k == pieces[i][0])
                def _(i=i):
                    weight_pass(i).wait()

            lax.fori_loop(0, nx, project, 0)

        @grouped(tau - picked - 6 * SLACK)
        def _(k0, n):
            second_all(k0, n).wait()
            for i in range(n):
                step_of(k0 + i)

        last = chunks + picked + SLACK

        for yy in range(ny):

            @pl.when(tau == last + yy)
            def _(yy=yy):
                def finish(zz, carry):
                    here = pl.ds(pl.multiple_of(yy * block + zz * cap, 8), cap)
                    value = proj[here, :]
                    hg[yy, zz] = (gcol[here, :][:, 0:1] * value).astype(BF)
                    term = jnp.sum(hid[yy, zz].astype(F32) * value, axis=1, keepdims=True)
                    hit = relr[yy, pl.ds(zz, 1), :] == spot_row
                    ret[yy, pl.ds(zz, 1), :] = jnp.sum(jnp.where(hit, term, 0.0), axis=0, keepdims=True)
                    return carry

                lax.fori_loop(0, nz, finish, 0)
                save_hg(yy).start()

        @pl.when(tau == last + ny - 1)
        def _():
            for j in range(1, ny):
                ret_copy(j).start()
            retr[y] = ret[y]

        @pl.when(tau == last + ny)
        def _():
            ret_all().wait()
            bz[...] = jnp.zeros_like(bz)
            for zz in range(nz):
                for yy in range(ny):
                    bz[zz, yy : yy + 1, :] = retr[yy, zz : zz + 1, :]
            for j in range(1, nz):
                back_copy(j).start()
            bk[z] = bz[z]

        @pl.when(tau == last + ny + 1)
        def _():
            back_all().wait()
            total = jnp.zeros(gg.shape, F32)
            for s in range(nz * ny):
                total = total + chosen[s] * bk[s // ny, s % ny : s % ny + 1, :]
            gg[...] = total

        return carry

    lax.fori_loop(0, chunks + picked + max(6 * SLACK, SLACK + ny + 2), step, 0)
    for k in range(chunks):
        for copy in saves(k):
            copy.wait()
    for yy in range(ny):
        save_hg(yy).wait()


def whole(nx, ny, nz, chunks, holder, route, pick, prob, tok, hid, mas, fst, snd):
    toks, feats = tok.shape
    dk = feats // chunks
    shard = mas.shape[0]
    cap, units = hid.shape[2:]
    slots = nz * ny
    count = slots * cap
    block = nz * cap
    part = shard // nz
    top = route.shape[0]
    hbm = pl.BlockSpec(memory_space=pl.ANY)
    vmem = pl.BlockSpec(memory_space=pltpu.VMEM)
    dma = pltpu.SemaphoreType.DMA
    n_dma = lambda *s: dma(tuple(max(1, v) for v in s))
    scratch = [
        pltpu.VMEM((ny, nz, cap, units), BF),
        pltpu.VMEM((shard, feats), F32),
        pltpu.VMEM((shard, feats), BF),
        pltpu.VMEM((shard, feats), BF),
        pltpu.VMEM((ny, nz, cap, units), BF),
        pltpu.VMEM((shard, feats), F32),
        pltpu.VMEM((shard, feats), BF),
        pltpu.VMEM((shard, feats), BF),
        pltpu.VMEM((slots, top, toks), F32),
        pltpu.VMEM((slots, toks), F32),
        pltpu.VMEM((nz, 8, toks), F32),
        pltpu.VMEM((chunks, nz, toks, dk), BF),
        pltpu.VMEM((chunks, CORES, nx, shard, dk), BF),
        pltpu.VMEM((nz // 2 + SLACK, ny, block, dk), BF),
        pltpu.VMEM((chunks, ny, block, dk), BF),
        pltpu.VMEM((nz // 2, ny * 2 * cap, 2 * toks), BF),
        pltpu.VMEM((count, 128), F32),
        pltpu.VMEM((CORES, units // CORES, count), BF),
        pltpu.VMEM((count, units), F32),
        pltpu.VMEM((SLACK, nx, shard, dk), BF),
        pltpu.VMEM((chunks, nx, shard, dk), BF),
        pltpu.VMEM((SLACK, nx, shard, dk), BF),
        pltpu.VMEM((SLACK, nx, shard, dk), BF),
        pltpu.VMEM((chunks, nx, shard, dk), BF),
        pltpu.VMEM((SLACK, shard, dk), F32),
        pltpu.VMEM((chunks, shard, dk), F32),
        pltpu.VMEM((chunks, nz, part, dk), BF),
        pltpu.VMEM((chunks, nz, part, dk), BF),
        pltpu.VMEM((chunks, HOT, part, dk), BF),
        pltpu.VMEM((chunks, ny, HOT, part, dk), BF),
        pltpu.VMEM((chunks, nz, part, dk), BF),
        pltpu.VMEM((chunks, nz, part, dk), BF),
        pltpu.VMEM((nz, 8, 128), F32),
        pltpu.VMEM((ny, 2 * nz, 128), F32),
        pltpu.VMEM((ny, 2 * nz, 128), F32),
        pltpu.VMEM((ny, nz, 128), F32),
        pltpu.VMEM((ny, nz, 128), F32),
        pltpu.VMEM((nz, 8, 128), F32),
        pltpu.VMEM((nz, 8, 128), F32),
        n_dma(chunks),
        n_dma(chunks),
        n_dma(2),
        n_dma(ny),
        n_dma(3, chunks),
        n_dma(ny),
        n_dma(2, nz // 2, chunks),
        n_dma(2, nz // 2, chunks),
        n_dma(chunks),
        n_dma(chunks),
        n_dma(chunks),
        n_dma(chunks),
        n_dma(chunks),
        n_dma(chunks),
        n_dma(chunks),
        n_dma(chunks),
        n_dma(chunks),
        n_dma(chunks),
        n_dma(chunks),
        n_dma(chunks),
        n_dma(chunks),
        n_dma(chunks),
        n_dma(chunks),
        n_dma(chunks),
        n_dma(1),
        n_dma(1),
        n_dma(1),
        n_dma(1),
        n_dma(1),
        n_dma(1),
        n_dma(1),
        n_dma(1),
    ]
    return pl.pallas_call(
        functools.partial(kernel, nx, ny, nz, chunks, cap),
        out_shape=(
            jax.ShapeDtypeStruct((nz, ny, cap, units), BF),
            jax.ShapeDtypeStruct((top, toks), F32),
            jax.ShapeDtypeStruct((shard, feats), F32),
            jax.ShapeDtypeStruct((shard, feats), BF),
            jax.ShapeDtypeStruct((shard, feats), BF),
        ),
        in_specs=[pl.BlockSpec(memory_space=pltpu.SMEM), vmem, vmem, vmem, hbm, hbm, hbm, hbm, hbm],
        out_specs=(hbm, vmem, hbm, hbm, hbm),
        scratch_shapes=scratch,
        compiler_params=pltpu.CompilerParams(
            collective_id=0, has_side_effects=True, vmem_limit_bytes=62 * 2**20
        ),
        cost_estimate=pl.CostEstimate(
            flops=4 * count * units * feats, bytes_accessed=20 * 2**20, transcendentals=0
        ),
    )(holder, route, pick, prob, tok, hid, mas, fst, snd)


def on_device(
    nx,
    ny,
    nz,
    chunks,
    grad_out,
    gate_probs,
    expert_route,
    replica_pick,
    slot_expert,
    saved_hidden,
    master,
    first_moment,
    second_moment,
):
    cap, units = saved_hidden.shape[4:]
    hidden_grad, gate_grad, new_master, new_first, new_second = whole(
        nx,
        ny,
        nz,
        chunks,
        slot_expert,
        expert_route.T,
        replica_pick.T,
        gate_probs.T,
        grad_out,
        saved_hidden.reshape(nz, ny, cap, units),
        master[0],
        first_moment[0],
        second_moment[0],
    )
    return (
        hidden_grad.reshape(saved_hidden.shape),
        gate_grad.T,
        new_master[None],
        new_first[None],
        new_second[None],
    )


def build(mesh, nx, ny, nz, chunks):
    tokens = P(("dp", "expert"), None)
    acts = P("dp", "expert", None, None, None, None)
    shard = P("expert", "dp", None)
    return jax.shard_map(
        functools.partial(on_device, nx, ny, nz, chunks),
        mesh=mesh,
        in_specs=(tokens, tokens, tokens, tokens, P(), acts, shard, shard, shard),
        out_specs=(acts, tokens, shard, shard, shard),
        check_vma=False,
    )


def solution(mesh):
    ny = 4
    return build(mesh, mesh.shape["dp"] // CORES, ny, mesh.shape["expert"] // ny, 7)
```
